32 devices in a mesh: ctx: 8 (over z, x), head: 4 (over y, core).
Axes of the slice: x: 2, y: 2, z: 4, core: 2. Of those that a mesh axis runs over, the one named last changes fastest.
Arguments:
- query_proj: bfloat16 [1024, 4096], P('ctx', 'head'), may hold values from -6 to 6
- key_proj: bfloat16 [1024, 4096], P('ctx', 'head'), may hold values from -0.375 to 0.375
- value_proj: bfloat16 [1024, 8192], P('ctx', 'head'), may hold values from -6 to 6
- gate_proj: bfloat16 [1024, 8192], P('ctx', 'head'), may hold values from -6 to 6
- decay_log: float32 [16, 1024], P('head', 'ctx'), may hold values from -1 to 0
- out_weight: bfloat16 [8192, 4096], P('head'), may hold values from -0.0625 to 0.0625
Outputs:
- layer_out: bfloat16 [1024, 4096], P(('ctx', 'head'))
The draws below stay inside these ranges and needn't reach their ends.
All inputs are finite; a program needn't handle non-finite values.
Results may differ from the reference program's by a relative error of at most 0.023.
Values may be sent and summed in bfloat16 or wider, within the bound.
No kernel may reach another device: no remote copies, remote signals or barrier semaphores. Data moves between devices by JAX's collectives and lax.ppermute only.
A program may use at most 128 MiB of HBM per device.

```python
import math
import jax
import jax.numpy as jnp
from jax import lax

D = 4096
RETENTION_HEADS = 16
KD = 256
VD = 512
TOK_DEV = 128
WINDOW_TOKENS = 1024


def draw_decay_log(key, part):
    random_subkeys = jax.random.split(jax.random.fold_in(key, 17), 6)
    fast_share = 5
    fast_heads = jax.random.randint(random_subkeys[0], (RETENTION_HEADS, 1), 0, 10) < fast_share
    fast_rate = jnp.exp(jax.random.uniform(random_subkeys[1], (RETENTION_HEADS, 1), jnp.float32, math.log(1.0 / 50.0), math.log(1.0 / 30.0)))
    slow_rate = jnp.exp(jax.random.uniform(random_subkeys[2], (RETENTION_HEADS, 1), jnp.float32, math.log(2.0 ** (-20)), math.log(0.5 / WINDOW_TOKENS)))
    baseline_decay_rate = jnp.where(fast_heads, fast_rate, slow_rate)
    decay_jitter_scale = jnp.exp(jax.random.uniform(random_subkeys[3], (RETENTION_HEADS, WINDOW_TOKENS), jnp.float32, math.log(0.5), math.log(2.0)))
    spike_token_index = jax.random.randint(random_subkeys[4], (RETENTION_HEADS, 2, 1), 0, WINDOW_TOKENS)
    token_positions = jnp.arange(WINDOW_TOKENS, dtype=jnp.int32)[None, None, :]
    spike_token_flag = jnp.any(spike_token_index == token_positions, axis=1)
    spike_decay_drop = jax.random.uniform(random_subkeys[5], (RETENTION_HEADS, WINDOW_TOKENS), jnp.float32, -0.6, -0.22)
    return (-baseline_decay_rate * decay_jitter_scale + jnp.where(spike_token_flag, spike_decay_drop, 0.0)).astype(jnp.float32)


def block_scale(stream_key, extent, shards, least, largest):
    gain, own = 1.0, jax.random.fold_in(stream_key, 6)
    for position, shards_of in shards:
        heights = jnp.exp(jax.random.uniform(jax.random.fold_in(own, position), (shards_of,), jnp.float32, least / len(shards), largest / len(shards)))
        gain = gain * jnp.repeat(heights, extent[position] // shards_of).reshape([-1 if axis == position else 1 for axis in range(len(extent))])
    return gain


def normal_values(own_key, dims, deviation, reach, cuts=(), kind=jnp.bfloat16):
    result = deviation * jax.random.normal(own_key, dims, jnp.float32)
    if cuts:
        result = result * block_scale(own_key, dims, cuts, -0.22, 0.18)
    return jnp.clip(result, -reach, reach).astype(kind)


def setup_inputs(seed: int = 0) -> dict:
    splits = jax.random.split(jax.random.key(seed), 7)
    query_proj = normal_values(splits[0], (WINDOW_TOKENS, RETENTION_HEADS * KD), 1.0, 6.0, ((0, 8), (1, 4)))
    key_proj = normal_values(splits[1], (WINDOW_TOKENS, RETENTION_HEADS * KD), KD ** -0.5, 0.375, ((0, 8), (1, 4)))
    value_proj = normal_values(splits[2], (WINDOW_TOKENS, RETENTION_HEADS * VD), 1.0, 6.0, ((0, 8), (1, 4)))
    gate_proj = normal_values(splits[3], (WINDOW_TOKENS, RETENTION_HEADS * VD), 1.0, 6.0, ((0, 8), (1, 4)))
    decay_log = draw_decay_log(jax.random.fold_in(splits[6], 71), 0)
    out_weight = normal_values(splits[5], (RETENTION_HEADS * VD, D), (RETENTION_HEADS * VD) ** -0.5, 0.0625, ((0, 4),))
    return {"query_proj": query_proj, "key_proj": key_proj, "value_proj": value_proj, "gate_proj": gate_proj, "decay_log": decay_log, "out_weight": out_weight}


def reference(query_proj, key_proj, value_proj, gate_proj, decay_log, out_weight):
    block_total = WINDOW_TOKENS // TOK_DEV
    token_positions = jnp.arange(TOK_DEV, dtype=jnp.int32)
    causal = (token_positions[:, None] >= token_positions[None, :])[None, :, :]

    def scan_step(carried_over_state, block_index):
        row_start = (block_index * TOK_DEV).astype(jnp.int32)
        query_heads = lax.dynamic_slice_in_dim(query_proj, row_start, TOK_DEV, 0).reshape(TOK_DEV, RETENTION_HEADS, KD).astype(jnp.float32)
        key_heads = lax.dynamic_slice_in_dim(key_proj, row_start, TOK_DEV, 0).reshape(TOK_DEV, RETENTION_HEADS, KD)
        value_head_rows = lax.dynamic_slice_in_dim(value_proj, row_start, TOK_DEV, 0).reshape(TOK_DEV, RETENTION_HEADS, VD).astype(jnp.float32)
        gate_heads = lax.dynamic_slice_in_dim(gate_proj, row_start, TOK_DEV, 0).reshape(TOK_DEV, RETENTION_HEADS, VD).astype(jnp.float32)
        decay_here = lax.dynamic_slice_in_dim(decay_log, row_start, TOK_DEV, 1)
        local_sum = jnp.cumsum(decay_here, axis=1)
        block_end = local_sum[:, -1:]
        gap_matrix = local_sum[:, :, None] - local_sum[:, None, :]
        decay_table = jnp.where(causal, jnp.exp(jnp.where(causal, gap_matrix, 0.0)), 0.0)
        scores = jnp.einsum('thk,shk->hts', query_heads, key_heads.astype(jnp.float32), precision=lax.Precision.HIGHEST)
        weights = (scores * decay_table).astype(jnp.bfloat16)
        inner_part = jnp.einsum('hts,shv->thv', weights.astype(jnp.float32), value_head_rows, precision=lax.Precision.HIGHEST)
        key_scale = jnp.exp(block_end - local_sum).T
        key_weighted_rows = (key_heads.astype(jnp.float32) * key_scale[:, :, None]).astype(jnp.bfloat16)
        running_block_state = jnp.einsum('cat,cad->atd', key_weighted_rows.astype(jnp.float32), value_head_rows, precision=lax.Precision.HIGHEST)
        block_decay = jnp.exp(block_end[:, 0])
        scaled_query_rows = query_heads * jnp.exp(local_sum).T[:, :, None]
        carried_state_term = jnp.einsum('mgo,goi->mgi', scaled_query_rows, carried_over_state, precision=lax.Precision.HIGHEST)
        retained = inner_part + carried_state_term
        row_mean = lax.optimization_barrier(jnp.mean(retained, axis=2, keepdims=True))
        centered = retained - row_mean
        row_var = lax.optimization_barrier(jnp.mean(centered * centered, axis=2, keepdims=True))
        normed = centered * lax.rsqrt(row_var + 1e-05)
        mixed_rows = (normed * jax.nn.silu(gate_heads)).astype(jnp.bfloat16).reshape(TOK_DEV, RETENTION_HEADS * VD)
        block_out = jnp.dot(mixed_rows, out_weight, preferred_element_type=jnp.float32).astype(jnp.bfloat16)
        next_state = carried_over_state * block_decay[:, None, None] + running_block_state
        return (next_state, block_out)
    empty_state = jnp.zeros((RETENTION_HEADS, KD, VD), jnp.float32)
    _, stacked = lax.scan(scan_step, empty_state, jnp.arange(block_total, dtype=jnp.int32))
    return stacked.reshape(WINDOW_TOKENS, D)
```

```python
import functools
import jax
import jax.numpy as jnp
from jax import lax
from jax.experimental import pallas as pl
from jax.experimental.pallas import tpu as pltpu
from jax.sharding import PartitionSpec as P

F32 = jnp.float32
BF16 = jnp.bfloat16
TAIL = 16
SMEM = pl.BlockSpec(memory_space=pltpu.SMEM)
VMEM = pl.BlockSpec(memory_space=pltpu.VMEM)


def params(mib):
    return pltpu.CompilerParams(vmem_limit_bytes=mib * 2**20)


def cost(flops, bytes_accessed):
    return pl.CostEstimate(flops=flops, bytes_accessed=bytes_accessed, transcendentals=0)


def iotas(rows):
    down = lax.broadcasted_iota(jnp.int32, (rows, rows), 0)
    across = lax.broadcasted_iota(jnp.int32, (rows, rows), 1)
    return down, across


def lanes(ref, index, width):
    return ref[:, pl.ds(pl.multiple_of(index * width, width), width)]


def pack_kernel(place_ref, decay_ref, key_ref, value_ref, *out_refs, key_dim, value_dim):
    rows = key_ref.shape[0]
    down, across = iotas(rows)
    for hop, out_ref in enumerate(out_refs):
        head = place_ref[0] ^ hop
        decay = decay_ref[pl.ds(head, 1), :]
        after = jnp.sum(jnp.where(across > down, decay, 0.0), axis=1, keepdims=True)
        keyed = lanes(key_ref, head, key_dim).astype(F32) * jnp.exp(after)
        out_ref[0:rows, :] = keyed.astype(BF16)
        values = lanes(value_ref, head, value_dim)
        for piece in range(value_dim // key_dim):
            out_ref[(piece + 1) * rows : (piece + 2) * rows, :] = values[
                :, piece * key_dim : (piece + 1) * key_dim
            ]
        whole = jnp.exp(jnp.sum(decay, axis=1, keepdims=True))
        whole = jnp.broadcast_to(whole, (TAIL, key_dim))
        high = whole.astype(BF16).astype(F32)
        middle = (whole - high).astype(BF16).astype(F32)
        low = whole - high - middle
        row = lax.broadcasted_iota(jnp.int32, (TAIL, key_dim), 0)
        tail = jnp.where(row == 0, high, jnp.where(row == 1, middle, jnp.where(row == 2, low, 0.0)))
        out_ref[out_ref.shape[0] - TAIL :, :] = tail.astype(BF16)


def query_kernel(place_ref, decay_ref, query_ref, *out_refs, key_dim):
    rows = query_ref.shape[0]
    down, across = iotas(rows)
    for hop, out_ref in enumerate(out_refs):
        head = place_ref[0] ^ hop
        decay = decay_ref[pl.ds(head, 1), :]
        upto = jnp.sum(jnp.where(across <= down, decay, 0.0), axis=1, keepdims=True)
        out_ref[...] = (lanes(query_ref, head, key_dim).astype(F32) * jnp.exp(upto)).astype(BF16)


def block_decay(message_ref):
    tail = message_ref[message_ref.shape[0] - TAIL :, :].astype(F32)
    return tail[0:1] + tail[1:2] + tail[2:3]


def block_state(message_ref, rows, piece):
    return lax.dot_general(
        message_ref[0:rows, :],
        message_ref[(piece + 1) * rows : (piece + 2) * rows, :],
        (((0,), (0,)), ((), ())),
        preferred_element_type=F32,
    )


def state_kernel(place_ref, *refs, rows):
    messages, (state_ref, whole_ref) = refs[:-2], refs[-2:]
    key_dim = messages[0].shape[1]
    place = place_ref[0]
    decays = [block_decay(message) for message in messages]
    scales = []
    for hop in range(len(messages)):
        scale = jnp.ones((1, key_dim), F32)
        for other in range(len(messages)):
            if other != hop:
                scale = scale * jnp.where((place ^ other) > (place ^ hop), decays[other], 1.0)
        scales.append(scale)
    for piece in range(state_ref.shape[1] // key_dim):
        total = None
        for hop, message in enumerate(messages):
            term = block_state(message, rows, piece) * scales[hop]
            total = term if total is None else total + term
        state_ref[:, piece * key_dim : (piece + 1) * key_dim] = total.astype(state_ref.dtype)
    whole = decays[0]
    for decay in decays[1:]:
        whole = whole * decay
    whole_ref[...] = jnp.broadcast_to(whole, whole_ref.shape)


def group_kernel(place_ref, *refs, rows):
    count = (len(refs) - 5) // 2
    messages, queries = refs[:count], refs[count : 2 * count]
    part_ref, scaled_ref, states, earlier, decays = refs[2 * count :]
    key_dim = messages[0].shape[1]
    pieces = part_ref.shape[1] // key_dim
    place = place_ref[0]
    for hop, message in enumerate(messages):
        decays[place ^ hop] = jnp.broadcast_to(block_decay(message), decays.shape[1:])
        for piece in range(pieces):
            states[place ^ hop, :, piece * key_dim : (piece + 1) * key_dim] = block_state(message, rows, piece)
    whole = jnp.ones((1, key_dim), F32)
    for block in range(count):
        if block == 0:
            earlier[0] = jnp.zeros(earlier.shape[1:], BF16)
        elif block == 1:
            total = states[0]
            earlier[1] = total.astype(BF16)
        else:
            total = total * jnp.concatenate([decay] * pieces, axis=1) + states[block - 1]
            earlier[block] = total.astype(BF16)
        decay = decays[block][0:1]
        decays[block] = jnp.broadcast_to(whole, decays.shape[1:])
        whole = whole * decay
    for hop, query in enumerate(queries):
        block = place ^ hop
        part_ref[hop * rows : (hop + 1) * rows, :] = jnp.dot(
            query[...], earlier[block], preferred_element_type=F32
        )
        scaled_ref[hop * rows : (hop + 1) * rows, :] = (query[...].astype(F32) * decays[block][0:1]).astype(BF16)


def cross_kernel(state_ref, scaled_ref, part_ref, *out_refs):
    rows = out_refs[0].shape[0]
    total = part_ref[...] + jnp.dot(scaled_ref[...], state_ref[...], preferred_element_type=F32)
    for hop, out_ref in enumerate(out_refs):
        out_ref[...] = total[hop * rows : (hop + 1) * rows, :].astype(BF16)


def inner_kernel(decay_ref, query_ref, key_ref, value_ref, gate_ref, inner_ref, swish_ref, *, key_dim, value_dim):
    rows = query_ref.shape[0]
    down, across = iotas(rows)
    for head in range(decay_ref.shape[0]):
        decay = decay_ref[head : head + 1, :]
        column = jnp.sum(jnp.where(across <= down, decay, 0.0), axis=1, keepdims=True)
        diagonal = jnp.where(across == down, column, 0.0)
        line = jnp.sum(diagonal, axis=0, keepdims=True)
        causal = across <= down
        table = jnp.where(causal, jnp.exp(jnp.where(causal, column - line, 0.0)), 0.0)
        keys = slice(head * key_dim, (head + 1) * key_dim)
        features = slice(head * value_dim, (head + 1) * value_dim)
        scores = lax.dot_general(
            query_ref[:, keys], key_ref[:, keys], (((1,), (1,)), ((), ())), preferred_element_type=F32
        )
        inner_ref[:, features] = jnp.dot(
            (scores * table).astype(BF16), value_ref[:, features], preferred_element_type=F32
        )
        gate = gate_ref[:, features].astype(F32)
        swish_ref[:, features] = gate / (1.0 + jnp.exp(-gate))


def project_kernel(place_ref, inner_ref, swish_ref, *refs, owners):
    weight_ref, send_ref, keep_ref, mixed, left = refs[-5:]
    parts = refs[:-5]
    rows, value_dim = parts[0].shape
    half = send_ref.shape[0]

    @pl.when(pl.program_id(0) == 0)
    def _():
        place, owner = place_ref[0], place_ref[1]
        for hop, part in enumerate(parts):
            head = place ^ hop
            retained = lanes(inner_ref, head, value_dim) + part[...].astype(F32)
            mean = jnp.mean(retained, axis=1, keepdims=True)
            centered = retained - mean
            variance = jnp.mean(centered * centered, axis=1, keepdims=True)
            mixed[:, pl.ds(pl.multiple_of(head * value_dim, value_dim), value_dim)] = (
                centered * lax.rsqrt(variance + 1e-05) * lanes(swish_ref, head, value_dim)
            )
        share = rows // owners
        bits = owners.bit_length() - 1
        pieces = []
        for position in range(owners):
            flipped = owners - 1 - position
            mask = sum(((flipped >> bit) & 1) << (bits - 1 - bit) for bit in range(bits))
            start = pl.multiple_of((owner ^ mask) * share, share)
            pieces.append(mixed[pl.ds(start, share), :])
        left[...] = jnp.concatenate(pieces, axis=0).astype(BF16)

    out = jnp.dot(left[...], weight_ref[...], preferred_element_type=F32)
    send_ref[...] = out[:half].astype(BF16)
    keep_ref[...] = out[half:].astype(BF16)


def swap(value, axis, size, mask):
    return lax.ppermute(value, axis, [(i, i ^ mask) for i in range(size)])


def carried_into(state, whole, axis, size, group):
    def shift(value, by):
        return lax.ppermute(value, axis, [(i, i + by * group) for i in range(size - by * group)])

    groups = size // group
    if groups == 1:
        return jnp.zeros_like(state)
    got = shift(state, 1)
    if groups == 2:
        return got
    first = lax.axis_index(axis) < group
    total, product = got.astype(F32), jnp.where(first, 1.0, shift(whole, 1))
    by = 1
    pieces = state.shape[1] // whole.shape[1]
    while by < groups - 1:
        none = lax.axis_index(axis) < by * group
        earlier, before = shift(total.astype(BF16), by), jnp.where(none, 1.0, shift(product, by))
        total = total + jnp.tile(product[0:1], (1, pieces)) * earlier.astype(F32)
        product = product * before
        by *= 2
    return total.astype(BF16)


def local(query, key, value, gate, decay, weight, *, ctx, head):
    rows = query.shape[0]
    heads = decay.shape[0]
    key_dim = query.shape[1] // heads
    value_dim = value.shape[1] // heads
    width = weight.shape[1]
    group = heads
    me = lax.axis_index("ctx")
    place = (me % group).astype(jnp.int32).reshape(1)
    both = jnp.stack([me % group, lax.axis_index("head")]).astype(jnp.int32)

    message = jax.ShapeDtypeStruct((rows * (1 + value_dim // key_dim) + TAIL, key_dim), BF16)
    messages = pl.pallas_call(
        functools.partial(pack_kernel, key_dim=key_dim, value_dim=value_dim),
        out_shape=[message] * group,
        in_specs=[SMEM, VMEM, VMEM, VMEM],
        out_specs=[VMEM] * group,
        compiler_params=params(16),
        name="pack_keys_values",
    )(place, decay, key, value)
    messages = [messages[0]] + [swap(messages[hop], "ctx", ctx, hop) for hop in range(1, group)]

    state, whole = pl.pallas_call(
        functools.partial(state_kernel, rows=rows),
        out_shape=[
            jax.ShapeDtypeStruct((key_dim, value_dim), BF16),
            jax.ShapeDtypeStruct((8, key_dim), F32),
        ],
        in_specs=[SMEM] + [VMEM] * group,
        out_specs=[VMEM] * 2,
        compiler_params=params(16),
        name="group_state",
    )(place, *messages)
    carried = carried_into(state, whole, "ctx", ctx, group)

    query_after, _ = lax.optimization_barrier((query, state))
    queries = pl.pallas_call(
        functools.partial(query_kernel, key_dim=key_dim),
        out_shape=[jax.ShapeDtypeStruct((rows, key_dim), BF16)] * group,
        in_specs=[SMEM, VMEM, VMEM],
        out_specs=[VMEM] * group,
        compiler_params=params(16),
        name="pack_queries",
    )(place, decay, query_after)
    queries = [queries[0]] + [swap(queries[hop], "ctx", ctx, hop) for hop in range(1, group)]

    inner, swish = pl.pallas_call(
        functools.partial(inner_kernel, key_dim=key_dim, value_dim=value_dim),
        out_shape=[jax.ShapeDtypeStruct(value.shape, F32)] * 2,
        in_specs=[VMEM] * 5,
        out_specs=[VMEM] * 2,
        compiler_params=params(24),
        cost_estimate=cost(10**9, 4 * 2**20),
        name="block_part",
    )(decay, query_after, key, value, gate)

    part, scaled = pl.pallas_call(
        functools.partial(group_kernel, rows=rows),
        out_shape=[
            jax.ShapeDtypeStruct((group * rows, value_dim), F32),
            jax.ShapeDtypeStruct((group * rows, key_dim), BF16),
        ],
        in_specs=[SMEM] + [VMEM] * (2 * group),
        out_specs=[VMEM] * 2,
        scratch_shapes=[
            pltpu.VMEM((group, key_dim, value_dim), F32),
            pltpu.VMEM((group, key_dim, value_dim), BF16),
            pltpu.VMEM((group, 8, key_dim), F32),
        ],
        compiler_params=params(24),
        cost_estimate=cost(10**9, 4 * 2**20),
        name="group_part",
    )(place, *messages, *queries)

    parts = pl.pallas_call(
        cross_kernel,
        out_shape=[jax.ShapeDtypeStruct((rows, value_dim), BF16)] * group,
        in_specs=[VMEM] * 3,
        out_specs=[VMEM] * group,
        compiler_params=params(16),
        name="carried_part",
    )(carried, scaled, part)
    parts = [parts[0]] + [swap(parts[hop], "ctx", ctx, hop) for hop in range(1, group)]

    tile = 512
    half = rows // 2
    fixed = lambda i: (0, 0)
    send, keep = pl.pallas_call(
        functools.partial(project_kernel, owners=head),
        out_shape=[jax.ShapeDtypeStruct((half, width), BF16)] * 2,
        grid=(width // tile,),
        in_specs=[SMEM]
        + [pl.BlockSpec(value.shape, fixed)] * 2
        + [pl.BlockSpec((rows, value_dim), fixed)] * group
        + [pl.BlockSpec((weight.shape[0], tile), lambda i: (0, i))],
        out_specs=[pl.BlockSpec((half, tile), lambda i: (0, i))] * 2,
        scratch_shapes=[pltpu.VMEM(value.shape, F32), pltpu.VMEM(value.shape, BF16)],
        compiler_params=params(40),
        name="project",
    )(both, inner, swish, *parts, weight)

    mask = 1
    while mask < head:
        total = keep.astype(F32) + swap(send, "head", head, mask).astype(F32)
        half = total.shape[0] // 2
        send, keep = total[:half].astype(BF16), total[half:]
        mask *= 2
        if mask >= head:
            return total.astype(BF16)


def solution(mesh):
    in_specs = (
        P("ctx", "head"),
        P("ctx", "head"),
        P("ctx", "head"),
        P("ctx", "head"),
        P("head", "ctx"),
        P("head", None),
    )
    out_specs = P(("ctx", "head"), None)
    body = functools.partial(local, ctx=mesh.shape["ctx"], head=mesh.shape["head"])
    return jax.shard_map(body, mesh=mesh, in_specs=in_specs, out_specs=out_specs, check_vma=False)
```

```python
import functools
import jax
import jax.numpy as jnp
from jax import lax
from jax.experimental import pallas as pl
from jax.experimental.pallas import tpu as pltpu
from jax.sharding import PartitionSpec as P

F32 = jnp.float32
BF16 = jnp.bfloat16
TAIL = 16
PARTS = 4
SMEM = pl.BlockSpec(memory_space=pltpu.SMEM)
VMEM = pl.BlockSpec(memory_space=pltpu.VMEM)
HBM = pl.BlockSpec(memory_space=pltpu.HBM)


def params(mib):
    return pltpu.CompilerParams(vmem_limit_bytes=mib * 2**20)


def cost(flops, bytes_accessed):
    return pl.CostEstimate(flops=flops, bytes_accessed=bytes_accessed, transcendentals=0)


def in_hbm(*values):
    return [pltpu.with_memory_space_constraint(value, pltpu.HBM) for value in values]


def iotas(rows):
    down = lax.broadcasted_iota(jnp.int32, (rows, rows), 0)
    across = lax.broadcasted_iota(jnp.int32, (rows, rows), 1)
    return down, across


def features(index, width):
    return pl.ds(pl.multiple_of(index * width, width), width)


def fetch(pairs, sems):
    copies = [pltpu.make_async_copy(src, dst, sems.at[i]) for i, (src, dst) in enumerate(pairs)]
    for copy in copies:
        copy.start()
    return copies


def pack_kernel(place_ref, owner_ref, decay_hbm, key_hbm, value_hbm, query_hbm, *refs):
    decay_ref, key_ref, query_ref, sems, value_sems = refs[-5:]
    count = (len(refs) - 5) // 2
    first, second = refs[:count], refs[count : 2 * count]
    rows, width = first[0].shape[0] // 2 - TAIL // 2, first[0].shape[1]
    place = place_ref[0] & (count - 1)
    head_copies = fetch([(decay_hbm, decay_ref), (key_hbm, key_ref), (query_hbm, query_ref)], sems)
    pairs = []
    for hop in range(count):
        head = place ^ hop
        pairs.append((value_hbm.at[:, features(2 * head, width)], first[hop].at[rows : 2 * rows]))
        pairs.append((value_hbm.at[:, features(2 * head + 1, width)], second[hop].at[0:rows]))
    value_copies = fetch(pairs, value_sems)
    down, across = iotas(rows)
    for copy in head_copies:
        copy.wait()
    for hop in range(count):
        head = place ^ hop
        decay = decay_ref[pl.ds(head, 1), :]
        after = jnp.sum(jnp.where(across > down, decay, 0.0), axis=1, keepdims=True)
        upto = jnp.sum(jnp.where(across <= down, decay, 0.0), axis=1, keepdims=True)
        keys = key_ref[:, features(head, width)].astype(F32)
        first[hop][0:rows, :] = (keys * jnp.exp(after)).astype(BF16)
        queries = query_ref[:, features(head, width)].astype(F32)
        second[hop][rows : 2 * rows, :] = (queries * jnp.exp(upto)).astype(BF16)
        whole = jnp.exp(jnp.sum(decay, axis=1, keepdims=True))
        whole = jnp.broadcast_to(whole, (TAIL, width))
        high = whole.astype(BF16).astype(F32)
        middle = (whole - high).astype(BF16).astype(F32)
        low = whole - high - middle
        row = lax.broadcasted_iota(jnp.int32, (TAIL, width), 0)
        tail = jnp.where(row == 0, high, jnp.where(row == 1, middle, jnp.where(row == 2, low, 0.0)))
        first[hop][2 * rows :, :] = tail.astype(BF16)
    for copy in value_copies:
        copy.wait()


def block_decay(message_ref):
    tail = message_ref[message_ref.shape[0] - TAIL :, :].astype(F32)
    return tail[0:1] + tail[1:2] + tail[2:3]


def outer(keys, values):
    return lax.dot_general(keys, values, (((0,), (0,)), ((), ())), preferred_element_type=F32)


def total_state(place, first, values, rows):
    decays = [block_decay(message) for message in first]
    total = None
    for hop, message in enumerate(first):
        scale = None
        for other in range(len(first)):
            if other != hop:
                factor = jnp.where((place ^ other) > (place ^ hop), decays[other], 1.0)
                scale = factor if scale is None else scale * factor
        term = outer(message[0:rows, :], values[hop])
        term = term if scale is None else term * scale
        total = term if total is None else total + term
    return total


def first_state_kernel(place_ref, *refs, rows):
    first, (state_ref, whole_ref) = refs[:-2], refs[-2:]
    values = [message[rows : 2 * rows, :] for message in first]
    state_ref[...] = total_state(place_ref[0] & (len(first) - 1), first, values, rows).astype(BF16)
    whole = block_decay(first[0])
    for message in first[1:]:
        whole = whole * block_decay(message)
    whole_ref[...] = jnp.broadcast_to(whole, whole_ref.shape)


def second_state_kernel(place_ref, *refs, rows):
    count = (len(refs) - 1) // 2
    first, second, state_ref = refs[:count], refs[count : 2 * count], refs[-1]
    values = [message[0:rows, :] for message in second]
    state_ref[...] = total_state(place_ref[0] & (len(first) - 1), first, values, rows).astype(BF16)


def group_kernel(place_ref, *refs, rows):
    count = (len(refs) - 6) // 2
    first, second = refs[:count], refs[count : 2 * count]
    left_ref, right_ref, scaled_ref, states, earlier, decays = refs[2 * count :]
    width = first[0].shape[1]
    place = place_ref[0] & (count - 1)
    for hop in range(count):
        block = place ^ hop
        decays[block] = jnp.broadcast_to(block_decay(first[hop]), decays.shape[1:])
        keys = first[hop][0:rows, :]
        states[block, :, 0:width] = outer(keys, first[hop][rows : 2 * rows, :])
        states[block, :, width : 2 * width] = outer(keys, second[hop][0:rows, :])
    whole = jnp.ones((1, width), F32)
    for block in range(count):
        if block == 0:
            earlier[0] = jnp.zeros(earlier.shape[1:], BF16)
        elif block == 1:
            total = states[0]
            earlier[1] = total.astype(BF16)
        else:
            total = total * jnp.concatenate([decay, decay], axis=1) + states[block - 1]
            earlier[block] = total.astype(BF16)
        decay = decays[block][0:1]
        decays[block] = jnp.broadcast_to(whole, decays.shape[1:])
        whole = whole * decay
    for hop in range(count):
        block = place ^ hop
        queries = second[hop][rows : 2 * rows, :]
        here = slice(hop * rows, (hop + 1) * rows)
        part = jnp.dot(queries, earlier[block], preferred_element_type=F32)
        left_ref[here, :] = part[:, 0:width]
        right_ref[here, :] = part[:, width : 2 * width]
        scaled_ref[here, :] = (queries.astype(F32) * decays[block][0:1]).astype(BF16)


def crossed(place_ref, state_ref, scaled_ref, part_ref, group):
    carried = jnp.dot(scaled_ref[...], state_ref[...], preferred_element_type=F32)
    return (part_ref[...] + jnp.where(place_ref[0] < group, 0.0, carried)).astype(BF16)


def left_cross_kernel(place_ref, state_ref, scaled_ref, part_ref, out_ref, *, group):
    out_ref[...] = crossed(place_ref, state_ref, scaled_ref, part_ref, group)


def right_cross_kernel(place_ref, state_ref, scaled_ref, part_ref, left_ref, *out_refs):
    rows, width = out_refs[0].shape
    right = crossed(place_ref, state_ref, scaled_ref, part_ref, len(out_refs))
    for hop, out_ref in enumerate(out_refs):
        here = slice(hop * rows, (hop + 1) * rows)
        out_ref[:, : width // 2] = left_ref[here, :]
        out_ref[:, width // 2 :] = right[here, :]


def block_kernel(*refs):
    decay_hbm, query_hbm, key_hbm, value_hbm, gate_hbm, inner_ref, swish_ref = refs[:7]
    decay_ref, query_ref, key_ref, value_ref, gate_ref, sems = refs[7:]
    rows = query_ref.shape[0]
    heads = decay_ref.shape[0]
    key_dim, value_dim = query_ref.shape[1] // heads, value_ref.shape[1] // heads
    copies = fetch(
        [
            (decay_hbm, decay_ref),
            (query_hbm, query_ref),
            (key_hbm, key_ref),
            (value_hbm, value_ref),
            (gate_hbm, gate_ref),
        ],
        sems,
    )
    down, across = iotas(rows)
    causal = across <= down
    for copy in copies:
        copy.wait()
    for head in range(heads):
        decay = decay_ref[head : head + 1, :]
        column = jnp.sum(jnp.where(causal, decay, 0.0), axis=1, keepdims=True)
        line = jnp.sum(jnp.where(across == down, column, 0.0), axis=0, keepdims=True)
        table = jnp.where(causal, jnp.exp(jnp.where(causal, column - line, 0.0)), 0.0)
        keys = slice(head * key_dim, (head + 1) * key_dim)
        here = slice(head * value_dim, (head + 1) * value_dim)
        scores = lax.dot_general(
            query_ref[:, keys], key_ref[:, keys], (((1,), (1,)), ((), ())), preferred_element_type=F32
        )
        inner_ref[:, here] = jnp.dot(
            (scores * table).astype(BF16), value_ref[:, here], preferred_element_type=F32
        )
        gate = gate_ref[:, here].astype(F32)
        swish_ref[:, here] = gate / (1.0 + jnp.exp(-gate))


def mix_kernel(place_ref, owner_ref, inner_ref, swish_ref, part_ref, out_ref, mixed, *, hop, group, owners):
    rows, value_dim = out_ref.shape
    here = features((place_ref[0] & (group - 1)) ^ hop, value_dim)
    retained = inner_ref[:, here] + part_ref[...].astype(F32)
    mean = jnp.mean(retained, axis=1, keepdims=True)
    centered = retained - mean
    variance = jnp.mean(centered * centered, axis=1, keepdims=True)
    mixed[...] = centered * lax.rsqrt(variance + 1e-05) * swish_ref[:, here]
    share = rows // owners
    bits = owners.bit_length() - 1
    pieces = []
    for position in range(owners):
        flipped = owners - 1 - position
        mask = sum(((flipped >> bit) & 1) << (bits - 1 - bit) for bit in range(bits))
        start = pl.multiple_of((owner_ref[0] ^ mask) * share, share)
        pieces.append(mixed[pl.ds(start, share), :])
    out_ref[...] = jnp.concatenate(pieces, axis=0).astype(BF16)


def project_kernel(place_ref, *refs, part):
    weight_ref, send_ref, keep_ref = refs[-3:]
    half, width = send_ref.shape
    place = place_ref[0] & (len(refs) - 4)
    tile = min(512, width)
    for start in range(0, width, tile):
        here = slice(start, start + tile)
        out = None
        for hop, rows_ref in enumerate(refs[:-3]):
            depth = rows_ref.shape[1]
            there = pl.ds(pl.multiple_of((place ^ hop) * depth, depth), depth)
            term = jnp.dot(rows_ref[...], weight_ref[there, slice(part * width + start, part * width + start + tile)], preferred_element_type=F32)
            out = term if out is None else out + term
        send_ref[:, here] = out[:half].astype(BF16)
        keep_ref[:, here] = out[half:].astype(BF16)


def swap(value, axis, size, mask):
    return lax.ppermute(value, axis, [(i, i ^ mask) for i in range(size)])


def swaps(values, axis, size):
    return [swap(values[hop], axis, size, hop) for hop in range(1, len(values))]


def carried_into(state, whole, axis, size, group, wrap):
    def shift(value, by):
        count = size if wrap else size - by * group
        return lax.ppermute(value, axis, [(i, (i + by * group) % size) for i in range(count)])

    groups = size // group
    if groups == 1:
        return state
    got = shift(state, 1)
    if groups == 2:
        return got
    first = lax.axis_index(axis) < group
    total, product = jnp.where(first, 0.0, got.astype(F32)), jnp.where(first, 1.0, shift(whole, 1))
    by = 1
    while by < groups - 1:
        none = lax.axis_index(axis) < by * group
        earlier, before = shift(total.astype(BF16), by), shift(product, by)
        total = total + jnp.where(none, 0.0, product[0:1] * earlier.astype(F32))
        product = product * jnp.where(none, 1.0, before)
        by *= 2
    return total.astype(BF16)


def reduce_over(send, keep, axis, size):
    keep = keep.astype(F32)
    mask = 1
    while mask < size:
        keep = keep + swap(send.astype(BF16), axis, size, mask).astype(F32)
        mask *= 2
        if mask < size:
            half = keep.shape[0] // 2
            send, keep = keep[:half], keep[half:]
    return keep.astype(BF16)


def local(query, key, value, gate, decay, weight, *, ctx, head):
    rows = query.shape[0]
    heads = decay.shape[0]
    key_dim = query.shape[1] // heads
    value_dim = value.shape[1] // heads
    depth, width = weight.shape
    group = heads
    me = lax.axis_index("ctx")
    place = me.astype(jnp.int32).reshape(1)
    owner = lax.axis_index("head").astype(jnp.int32).reshape(1)
    shape = jax.ShapeDtypeStruct

    packed = pl.pallas_call(
        pack_kernel,
        out_shape=[shape((2 * rows + TAIL, key_dim), BF16)] * group + [shape((2 * rows, key_dim), BF16)] * group,
        in_specs=[SMEM] * 2 + [HBM] * 4,
        out_specs=[VMEM] * (2 * group),
        scratch_shapes=[
            pltpu.VMEM(decay.shape, F32),
            pltpu.VMEM(key.shape, BF16),
            pltpu.VMEM(query.shape, BF16),
            pltpu.SemaphoreType.DMA((3,)),
            pltpu.SemaphoreType.DMA((2 * group,)),
        ],
        compiler_params=params(8),
        name="pack",
    )(place, owner, *in_hbm(decay, key, value, query))
    def after(value):
        return lax.optimization_barrier((decay, value))[0]

    token = after(packed[0])
    inner, swish = pl.pallas_call(
        block_kernel,
        out_shape=[shape(value.shape, F32)] * 2,
        in_specs=[HBM] * 5,
        out_specs=[VMEM] * 2,
        scratch_shapes=[
            pltpu.VMEM(decay.shape, F32),
            pltpu.VMEM(query.shape, BF16),
            pltpu.VMEM(key.shape, BF16),
            pltpu.VMEM(value.shape, BF16),
            pltpu.VMEM(gate.shape, BF16),
            pltpu.SemaphoreType.DMA((5,)),
        ],
        compiler_params=params(8),
        cost_estimate=cost(10**9, 4 * 2**20),
        name="block_part",
    )(*in_hbm(token, query, key, value, gate))

    first = swaps(packed[:group], "ctx", ctx)
    later, _ = lax.optimization_barrier((packed[group:], inner))
    second = [packed[group]] + swaps(later, "ctx", ctx)
    first = [packed[0]] + first
    left_state, whole = pl.pallas_call(
        functools.partial(first_state_kernel, rows=rows),
        out_shape=[shape((key_dim, key_dim), BF16), shape((8, key_dim), F32)],
        in_specs=[SMEM] + [VMEM] * group,
        out_specs=[VMEM] * 2,
        compiler_params=params(8),
        name="first_state",
    )(place, *first)
    left_carried = carried_into(left_state, whole, "ctx", ctx, group, True)

    right_state = pl.pallas_call(
        functools.partial(second_state_kernel, rows=rows),
        out_shape=shape((key_dim, key_dim), BF16),
        in_specs=[SMEM] + [VMEM] * (2 * group),
        out_specs=VMEM,
        compiler_params=params(8),
        name="second_state",
    )(place, *first, *second)
    right_carried = carried_into(right_state, whole, "ctx", ctx, group, False)

    left_part, right_part, scaled = pl.pallas_call(
        functools.partial(group_kernel, rows=rows),
        out_shape=[shape((group * rows, key_dim), F32)] * 2 + [shape((group * rows, key_dim), BF16)],
        in_specs=[SMEM] + [VMEM] * (2 * group),
        out_specs=[VMEM] * 3,
        scratch_shapes=[
            pltpu.VMEM((group, key_dim, value_dim), F32),
            pltpu.VMEM((group, key_dim, value_dim), BF16),
            pltpu.VMEM((group, 8, key_dim), F32),
        ],
        compiler_params=params(8),
        cost_estimate=cost(10**9, 4 * 2**20),
        name="group_part",
    )(place, *first, *second)

    left_cross = pl.pallas_call(
        functools.partial(left_cross_kernel, group=group),
        out_shape=shape((group * rows, key_dim), BF16),
        in_specs=[SMEM] + [VMEM] * 3,
        out_specs=VMEM,
        compiler_params=params(8),
        name="left_cross",
    )(place, left_carried, scaled, left_part)
    parts = pl.pallas_call(
        right_cross_kernel,
        out_shape=[shape((rows, value_dim), BF16)] * group,
        in_specs=[SMEM] + [VMEM] * 4,
        out_specs=[VMEM] * group,
        compiler_params=params(8),
        name="right_cross",
    )(place, right_carried, scaled, right_part, left_cross)
    parts = [parts[0]] + swaps(parts, "ctx", ctx)

    mixed_rows = [
        pl.pallas_call(
            functools.partial(mix_kernel, hop=hop, group=group, owners=head),
            out_shape=shape((rows, value_dim), BF16),
            in_specs=[SMEM] * 2 + [VMEM] * 3,
            out_specs=VMEM,
            scratch_shapes=[pltpu.VMEM((rows, value_dim), F32)],
            compiler_params=params(4),
            name="mix",
        )(place, owner, inner, swish, parts[hop])
        for hop in range(group)
    ]
    outs = []
    for part in range(PARTS):
        send, keep = pl.pallas_call(
            functools.partial(project_kernel, part=part),
            out_shape=[shape((rows // 2, width // PARTS), BF16)] * 2,
            in_specs=[SMEM] + [VMEM] * (group + 1),
            out_specs=[VMEM] * 2,
            compiler_params=params(4),
            cost_estimate=cost(2**29, 2**22),
            name="project",
        )(place, *mixed_rows, weight)
        outs.append(reduce_over(send, keep, "head", head))
    return jnp.concatenate(outs, axis=1)


def solution(mesh):
    in_specs = (
        P("ctx", "head"),
        P("ctx", "head"),
        P("ctx", "head"),
        P("ctx", "head"),
        P("head", "ctx"),
        P("head", None),
    )
    out_specs = P(("ctx", "head"), None)
    body = functools.partial(local, ctx=mesh.shape["ctx"], head=mesh.shape["head"])
    return jax.shard_map(body, mesh=mesh, in_specs=in_specs, out_specs=out_specs, check_vma=False)
```

```python
import functools
import jax
import jax.numpy as jnp
from jax import lax
from jax.experimental import pallas as pl
from jax.experimental.pallas import tpu as pltpu
from jax.sharding import PartitionSpec as P

F32 = jnp.float32
BF16 = jnp.bfloat16
TAIL = 16
PARTS = 2
SMEM = pl.BlockSpec(memory_space=pltpu.SMEM)
VMEM = pl.BlockSpec(memory_space=pltpu.VMEM)
HBM = pl.BlockSpec(memory_space=pltpu.HBM)


def params(mib):
    return pltpu.CompilerParams(vmem_limit_bytes=mib * 2**20)


def cost(flops, bytes_accessed):
    return pl.CostEstimate(flops=flops, bytes_accessed=bytes_accessed, transcendentals=0)


def in_hbm(*values):
    return [pltpu.with_memory_space_constraint(value, pltpu.HBM) for value in values]


def iotas(rows):
    down = lax.broadcasted_iota(jnp.int32, (rows, rows), 0)
    across = lax.broadcasted_iota(jnp.int32, (rows, rows), 1)
    return down, across


def features(index, width):
    return pl.ds(pl.multiple_of(index * width, width), width)


def fetch(pairs, sems):
    copies = [pltpu.make_async_copy(src, dst, sems.at[i]) for i, (src, dst) in enumerate(pairs)]
    for copy in copies:
        copy.start()
    return copies


def first_pack_kernel(place_ref, owner_ref, decay_hbm, key_hbm, value_hbm, *refs):
    decay_ref, key_ref, sems = refs[-3:]
    first = refs[:-3]
    count = len(first)
    rows, width = (first[0].shape[0] - TAIL) // 2, first[0].shape[1]
    place = place_ref[0] & (count - 1)
    pairs = [(decay_hbm, decay_ref), (key_hbm, key_ref)]
    for hop in range(count):
        pairs.append((value_hbm.at[:, features(2 * (place ^ hop), width)], first[hop].at[rows : 2 * rows]))
    copies = fetch(pairs, sems)
    down, across = iotas(rows)
    for copy in copies[:2]:
        copy.wait()
    for hop in range(count):
        head = place ^ hop
        decay = decay_ref[pl.ds(head, 1), :]
        after = jnp.sum(jnp.where(across > down, decay, 0.0), axis=1, keepdims=True)
        keys = key_ref[:, features(head, width)].astype(F32)
        first[hop][0:rows, :] = (keys * jnp.exp(after)).astype(BF16)
        whole = jnp.exp(jnp.sum(decay, axis=1, keepdims=True))
        whole = jnp.broadcast_to(whole, (TAIL, width))
        high = whole.astype(BF16).astype(F32)
        middle = (whole - high).astype(BF16).astype(F32)
        low = whole - high - middle
        row = lax.broadcasted_iota(jnp.int32, (TAIL, width), 0)
        tail = jnp.where(row == 0, high, jnp.where(row == 1, middle, jnp.where(row == 2, low, 0.0)))
        first[hop][2 * rows :, :] = tail.astype(BF16)
    for copy in copies[2:]:
        copy.wait()


def second_pack_kernel(place_ref, decay_hbm, query_hbm, value_hbm, *refs):
    decay_ref, query_ref, sems = refs[-3:]
    second = refs[:-3]
    count = len(second)
    rows, width = second[0].shape[0] // 2, second[0].shape[1]
    place = place_ref[0] & (count - 1)
    pairs = [(decay_hbm, decay_ref), (query_hbm, query_ref)]
    for hop in range(count):
        pairs.append((value_hbm.at[:, features(2 * (place ^ hop) + 1, width)], second[hop].at[0:rows]))
    copies = fetch(pairs, sems)
    down, across = iotas(rows)
    for copy in copies[:2]:
        copy.wait()
    for hop in range(count):
        head = place ^ hop
        decay = decay_ref[pl.ds(head, 1), :]
        upto = jnp.sum(jnp.where(across <= down, decay, 0.0), axis=1, keepdims=True)
        queries = query_ref[:, features(head, width)].astype(F32)
        second[hop][rows : 2 * rows, :] = (queries * jnp.exp(upto)).astype(BF16)
    for copy in copies[2:]:
        copy.wait()


def block_decay(message_ref):
    tail = message_ref[message_ref.shape[0] - TAIL :, :].astype(F32)
    return tail[0:1] + tail[1:2] + tail[2:3]


def outer(keys, values):
    return lax.dot_general(keys, values, (((0,), (0,)), ((), ())), preferred_element_type=F32)


def total_state(place, first, values, rows):
    decays = [block_decay(message) for message in first]
    total = None
    for hop, message in enumerate(first):
        scale = None
        for other in range(len(first)):
            if other != hop:
                factor = jnp.where((place ^ other) > (place ^ hop), decays[other], 1.0)
                scale = factor if scale is None else scale * factor
        term = outer(message[0:rows, :], values[hop])
        term = term if scale is None else term * scale
        total = term if total is None else total + term
    return total


def first_state_kernel(place_ref, *refs, rows):
    first, (state_ref, whole_ref) = refs[:-2], refs[-2:]
    values = [message[rows : 2 * rows, :] for message in first]
    state_ref[...] = total_state(place_ref[0] & (len(first) - 1), first, values, rows).astype(BF16)
    whole = block_decay(first[0])
    for message in first[1:]:
        whole = whole * block_decay(message)
    whole_ref[...] = jnp.broadcast_to(whole, whole_ref.shape)


def second_state_kernel(place_ref, *refs, rows):
    count = (len(refs) - 1) // 2
    first, second, state_ref = refs[:count], refs[count : 2 * count], refs[-1]
    values = [message[0:rows, :] for message in second]
    state_ref[...] = total_state(place_ref[0] & (len(first) - 1), first, values, rows).astype(BF16)


def group_kernel(place_ref, *refs, rows):
    count = (len(refs) - 6) // 2
    first, second = refs[:count], refs[count : 2 * count]
    left_ref, right_ref, scaled_ref, states, earlier, decays = refs[2 * count :]
    width = first[0].shape[1]
    place = place_ref[0] & (count - 1)
    for hop in range(count):
        block = place ^ hop
        decays[block] = jnp.broadcast_to(block_decay(first[hop]), decays.shape[1:])
        keys = first[hop][0:rows, :]
        states[block, :, 0:width] = outer(keys, first[hop][rows : 2 * rows, :])
        states[block, :, width : 2 * width] = outer(keys, second[hop][0:rows, :])
    whole = jnp.ones((1, width), F32)
    for block in range(count):
        if block == 0:
            earlier[0] = jnp.zeros(earlier.shape[1:], BF16)
        elif block == 1:
            total = states[0]
            earlier[1] = total.astype(BF16)
        else:
            total = total * jnp.concatenate([decay, decay], axis=1) + states[block - 1]
            earlier[block] = total.astype(BF16)
        decay = decays[block][0:1]
        decays[block] = jnp.broadcast_to(whole, decays.shape[1:])
        whole = whole * decay
    for hop in range(count):
        block = place ^ hop
        queries = second[hop][rows : 2 * rows, :]
        here = slice(hop * rows, (hop + 1) * rows)
        part = jnp.dot(queries, earlier[block], preferred_element_type=F32)
        left_ref[here, :] = part[:, 0:width]
        right_ref[here, :] = part[:, width : 2 * width]
        scaled_ref[here, :] = (queries.astype(F32) * decays[block][0:1]).astype(BF16)


def cross_kernel(place_ref, state_ref, scaled_ref, part_ref, *out_refs):
    rows = out_refs[0].shape[0]
    carried = jnp.dot(scaled_ref[...], state_ref[...], preferred_element_type=F32)
    total = part_ref[...] + jnp.where(place_ref[0] < len(out_refs), 0.0, carried)
    for hop, out_ref in enumerate(out_refs):
        out_ref[...] = total[hop * rows : (hop + 1) * rows, :].astype(BF16)


def block_kernel(*refs):
    decay_hbm, query_hbm, key_hbm, value_hbm, gate_hbm, inner_ref, swish_ref = refs[:7]
    decay_ref, query_ref, key_ref, value_ref, gate_ref, sems = refs[7:]
    rows = query_ref.shape[0]
    heads = decay_ref.shape[0]
    key_dim, value_dim = query_ref.shape[1] // heads, value_ref.shape[1] // heads
    copies = fetch(
        [
            (decay_hbm, decay_ref),
            (query_hbm, query_ref),
            (key_hbm, key_ref),
            (value_hbm, value_ref),
            (gate_hbm, gate_ref),
        ],
        sems,
    )
    down, across = iotas(rows)
    causal = across <= down
    for copy in copies:
        copy.wait()
    for head in range(heads):
        decay = decay_ref[head : head + 1, :]
        column = jnp.sum(jnp.where(causal, decay, 0.0), axis=1, keepdims=True)
        line = jnp.sum(jnp.where(across == down, column, 0.0), axis=0, keepdims=True)
        table = jnp.where(causal, jnp.exp(jnp.where(causal, column - line, 0.0)), 0.0)
        keys = slice(head * key_dim, (head + 1) * key_dim)
        here = slice(head * value_dim, (head + 1) * value_dim)
        scores = lax.dot_general(
            query_ref[:, keys], key_ref[:, keys], (((1,), (1,)), ((), ())), preferred_element_type=F32
        )
        inner_ref[:, here] = jnp.dot(
            (scores * table).astype(BF16), value_ref[:, here], preferred_element_type=F32
        )
        gate = gate_ref[:, here].astype(F32)
        swish_ref[:, here] = gate / (1.0 + jnp.exp(-gate))


def mix(place_ref, owner_ref, inner_ref, swish_ref, part_refs, mixed, hop, group, owners):
    rows, value_dim = mixed.shape
    here = features((place_ref[0] & (group - 1)) ^ hop, value_dim)
    part = jnp.concatenate([part_ref[...] for part_ref in part_refs], axis=1)
    retained = inner_ref[:, here] + part.astype(F32)
    mean = jnp.mean(retained, axis=1, keepdims=True)
    centered = retained - mean
    variance = jnp.mean(centered * centered, axis=1, keepdims=True)
    mixed[...] = centered * lax.rsqrt(variance + 1e-05) * swish_ref[:, here]
    share = rows // owners
    bits = owners.bit_length() - 1
    pieces = []
    for position in range(owners):
        flipped = owners - 1 - position
        mask = sum(((flipped >> bit) & 1) << (bits - 1 - bit) for bit in range(bits))
        start = pl.multiple_of((owner_ref[0] ^ mask) * share, share)
        pieces.append(mixed[pl.ds(start, share), :])
    return jnp.concatenate(pieces, axis=0).astype(BF16)


def head_product(place_ref, rows, weight_ref, hop, group, start, tile):
    depth = rows.shape[1]
    return jnp.dot(
        rows,
        weight_ref[features((place_ref[0] & (group - 1)) ^ hop, depth), start : start + tile],
        preferred_element_type=F32,
    )


def add_head_kernel(*refs, hop, group, owners):
    place_ref, owner_ref, inner_ref, swish_ref, weight_ref = refs[:5]
    before, part_refs = refs[5 : 5 + (hop > 0)], refs[5 + (hop > 0) : -2]
    total_ref, mixed = refs[-2:]
    rows = mix(place_ref, owner_ref, inner_ref, swish_ref, part_refs, mixed, hop, group, owners)
    width = total_ref.shape[1]
    tile = min(512, width)
    for start in range(0, width, tile):
        here = slice(start, start + tile)
        term = head_product(place_ref, rows, weight_ref, hop, group, start, tile)
        total_ref[:, here] = before[0][:, here] + term if before else term


def finish_part(place_ref, rows, weight_ref, totals, send_ref, keep_ref, part, late, group):
    half, width = send_ref.shape
    tile = min(512, width)
    for start in range(0, width, tile):
        here = slice(start, start + tile)
        there = part * width + start
        terms = [
            head_product(place_ref, rows_ref[...], weight_ref, hop, group, there, tile)
            for hop, rows_ref in zip(late, rows)
        ]
        terms += [total_ref[:, there : there + tile] for total_ref in totals]
        out = functools.reduce(jnp.add, terms)
        send_ref[:, here] = out[:half].astype(BF16)
        keep_ref[:, here] = out[half:].astype(BF16)


def first_part_kernel(*refs, late, group, owners):
    place_ref, owner_ref, inner_ref, swish_ref, weight_ref = refs[:5]
    count = len(late)
    totals, part_refs = refs[5 : 5 + (late[0] > 0)], refs[5 + (late[0] > 0) : -3 - count]
    send_ref, keep_ref, mixed = refs[-3 - count], refs[-2 - count], refs[-1]
    rows = refs[-1 - count : -1]
    each = len(part_refs) // count
    for at, (hop, rows_ref) in enumerate(zip(late, rows)):
        mine = part_refs[at * each : (at + 1) * each]
        rows_ref[...] = mix(place_ref, owner_ref, inner_ref, swish_ref, mine, mixed, hop, group, owners)
    finish_part(place_ref, rows, weight_ref, totals, send_ref, keep_ref, 0, late, group)


def other_part_kernel(place_ref, weight_ref, *refs, part, late, group):
    count = len(late)
    send_ref, keep_ref = refs[-2:]
    finish_part(place_ref, refs[:count], weight_ref, refs[count:-2], send_ref, keep_ref, part, late, group)


def swap(value, axis, size, mask):
    return lax.ppermute(value, axis, [(i, i ^ mask) for i in range(size)])


def swaps(values, axis, size):
    return [swap(values[hop], axis, size, hop) for hop in range(1, len(values))]


def carried_into(state, whole, axis, size, group):
    def shift(value, by):
        return lax.ppermute(value, axis, [(i, (i + by * group) % size) for i in range(size)])

    groups = size // group
    if groups == 1:
        return state
    got = shift(state, 1)
    if groups == 2:
        return got
    first = lax.axis_index(axis) < group
    total, product = jnp.where(first, 0.0, got.astype(F32)), jnp.where(first, 1.0, shift(whole, 1))
    by = 1
    while by < groups - 1:
        none = lax.axis_index(axis) < by * group
        earlier, before = shift(total.astype(BF16), by), shift(product, by)
        total = total + jnp.where(none, 0.0, product[0:1] * earlier.astype(F32))
        product = product * jnp.where(none, 1.0, before)
        by *= 2
    return total.astype(BF16)


def reduce_over(send, keep, axis, size):
    keep = keep.astype(F32)
    mask = 1
    while mask < size:
        keep = keep + swap(send.astype(BF16), axis, size, mask).astype(F32)
        mask *= 2
        if mask < size:
            half = keep.shape[0] // 2
            send, keep = keep[:half], keep[half:]
    return keep.astype(BF16)


def local(query, key, value, gate, decay, weight, *, ctx, head):
    rows = query.shape[0]
    heads = decay.shape[0]
    key_dim = query.shape[1] // heads
    value_dim = value.shape[1] // heads
    depth, width = weight.shape
    group = heads
    me = lax.axis_index("ctx")
    place = me.astype(jnp.int32).reshape(1)
    owner = lax.axis_index("head").astype(jnp.int32).reshape(1)
    shape = jax.ShapeDtypeStruct

    def after(value):
        return lax.optimization_barrier((decay, value))[0]

    first = pl.pallas_call(
        first_pack_kernel,
        out_shape=[shape((2 * rows + TAIL, key_dim), BF16)] * group,
        in_specs=[SMEM] * 2 + [HBM] * 3,
        out_specs=[VMEM] * group,
        scratch_shapes=[
            pltpu.VMEM(decay.shape, F32),
            pltpu.VMEM(key.shape, BF16),
            pltpu.SemaphoreType.DMA((2 + group,)),
        ],
        compiler_params=params(8),
        cost_estimate=cost(5 * 10**9, 2**24),
        name="first_pack",
    )(place, owner, *in_hbm(decay, key, value))
    second = pl.pallas_call(
        second_pack_kernel,
        out_shape=[shape((2 * rows, key_dim), BF16)] * group,
        in_specs=[SMEM] + [HBM] * 3,
        out_specs=[VMEM] * group,
        scratch_shapes=[
            pltpu.VMEM(decay.shape, F32),
            pltpu.VMEM(query.shape, BF16),
            pltpu.SemaphoreType.DMA((2 + group,)),
        ],
        compiler_params=params(8),
        name="second_pack",
    )(place, *in_hbm(after(first[0]), query, value))
    first = [first[0]] + swaps(first, "ctx", ctx)
    second = [second[0]] + swaps(second, "ctx", ctx)
    token = after(first[min(1, group - 1)])
    inner, swish = pl.pallas_call(
        block_kernel,
        out_shape=[shape(value.shape, F32)] * 2,
        in_specs=[HBM] * 5,
        out_specs=[VMEM] * 2,
        scratch_shapes=[
            pltpu.VMEM(decay.shape, F32),
            pltpu.VMEM(query.shape, BF16),
            pltpu.VMEM(key.shape, BF16),
            pltpu.VMEM(value.shape, BF16),
            pltpu.VMEM(gate.shape, BF16),
            pltpu.SemaphoreType.DMA((5,)),
        ],
        compiler_params=params(8),
        cost_estimate=cost(10**9, 4 * 2**20),
        name="block_part",
    )(*in_hbm(token, query, key, value, gate))

    first, inner = lax.optimization_barrier((first, inner))
    left_state, whole = pl.pallas_call(
        functools.partial(first_state_kernel, rows=rows),
        out_shape=[shape((key_dim, key_dim), BF16), shape((8, key_dim), F32)],
        in_specs=[SMEM] + [VMEM] * group,
        out_specs=[VMEM] * 2,
        compiler_params=params(8),
        cost_estimate=cost(5*10**9, 2**24),
        name="first_state",
    )(place, *first)
    left_carried = carried_into(left_state, whole, "ctx", ctx, group)

    right_state = pl.pallas_call(
        functools.partial(second_state_kernel, rows=rows),
        out_shape=shape((key_dim, key_dim), BF16),
        in_specs=[SMEM] + [VMEM] * (2 * group),
        out_specs=VMEM,
        compiler_params=params(8),
        cost_estimate=cost(5*10**9, 2**24),
        name="second_state",
    )(place, *first, *second)
    right_carried = carried_into(right_state, whole, "ctx", ctx, group)

    left_part, right_part, scaled = pl.pallas_call(
        functools.partial(group_kernel, rows=rows),
        out_shape=[shape((group * rows, key_dim), F32)] * 2 + [shape((group * rows, key_dim), BF16)],
        in_specs=[SMEM] + [VMEM] * (2 * group),
        out_specs=[VMEM] * 3,
        scratch_shapes=[
            pltpu.VMEM((group, key_dim, value_dim), F32),
            pltpu.VMEM((group, key_dim, value_dim), BF16),
            pltpu.VMEM((group, 8, key_dim), F32),
        ],
        compiler_params=params(8),
        cost_estimate=cost(10**9, 4 * 2**20),
        name="group_part",
    )(place, *first, *second)

    def cross(carried, part, name):
        parts = pl.pallas_call(
            cross_kernel,
            out_shape=[shape((rows, key_dim), BF16)] * group,
            in_specs=[SMEM] + [VMEM] * 3,
            out_specs=[VMEM] * group,
            compiler_params=params(8),
            name=name,
        )(place, carried, scaled, part)
        return [parts[0]] + swaps(parts, "ctx", ctx)

    left_parts = cross(left_carried, left_part, "left_cross")
    right_parts = cross(right_carried, right_part, "right_cross")
    inner, left_parts = lax.optimization_barrier((inner, left_parts))
    parts = list(zip(left_parts, right_parts))
    late = list(range(group))[-2:]
    total = []
    for hop in range(late[0]):
        total = [
            pl.pallas_call(
                functools.partial(add_head_kernel, hop=hop, group=group, owners=head),
                out_shape=shape((rows, width), F32),
                in_specs=[SMEM] * 2 + [VMEM] * (3 + len(total) + len(parts[hop])),
                out_specs=VMEM,
                input_output_aliases={5: 0} if total else {},
                scratch_shapes=[pltpu.VMEM((rows, value_dim), F32)],
                compiler_params=params(4),
                cost_estimate=cost(2**29, 2**22),
                name="add_head",
            )(place, owner, inner, swish, weight, *total, *parts[hop])
        ]
    late_parts = [piece for hop in late for piece in parts[hop]]
    outs = []
    halves = [shape((rows // 2, width // PARTS), BF16)] * 2
    for part in range(PARTS):
        if part == 0:
            send, keep, *last_rows = pl.pallas_call(
                functools.partial(first_part_kernel, late=late, group=group, owners=head),
                out_shape=halves + [shape((rows, value_dim), BF16)] * len(late),
                in_specs=[SMEM] * 2 + [VMEM] * (3 + len(total) + len(late_parts)),
                out_specs=[VMEM] * (2 + len(late)),
                scratch_shapes=[pltpu.VMEM((rows, value_dim), F32)],
                compiler_params=params(4),
                name="first_part",
            )(place, owner, inner, swish, weight, *total, *late_parts)
        else:
            send, keep = pl.pallas_call(
                functools.partial(other_part_kernel, part=part, late=late, group=group),
                out_shape=halves,
                in_specs=[SMEM] + [VMEM] * (1 + len(late) + len(total)),
                out_specs=[VMEM] * 2,
                compiler_params=params(4),
                name="other_part",
            )(place, weight, *last_rows, *total)
        outs.append(reduce_over(send, keep, "head", head))
    return jnp.concatenate(outs, axis=1)


def solution(mesh):
    in_specs = (
        P("ctx", "head"),
        P("ctx", "head"),
        P("ctx", "head"),
        P("ctx", "head"),
        P("head", "ctx"),
        P("head", None),
    )
    out_specs = P(("ctx", "head"), None)
    body = functools.partial(local, ctx=mesh.shape["ctx"], head=mesh.shape["head"])
    return jax.shard_map(body, mesh=mesh, in_specs=in_specs, out_specs=out_specs, check_vma=False)
```

```python
import functools
import jax
import jax.numpy as jnp
from jax import lax
from jax.experimental import pallas as pl
from jax.experimental.pallas import tpu as pltpu
from jax.sharding import PartitionSpec as P

F32 = jnp.float32
BF16 = jnp.bfloat16
TAIL = 16
SMEM = pl.BlockSpec(memory_space=pltpu.SMEM)
VMEM = pl.BlockSpec(memory_space=pltpu.VMEM)
HBM = pl.BlockSpec(memory_space=pltpu.HBM)


def params(mib):
    return pltpu.CompilerParams(vmem_limit_bytes=mib * 2**20)


def cost(flops, bytes_accessed):
    return pl.CostEstimate(flops=flops, bytes_accessed=bytes_accessed, transcendentals=0)


def in_hbm(*values):
    return [pltpu.with_memory_space_constraint(value, pltpu.HBM) for value in values]


def iotas(rows):
    down = lax.broadcasted_iota(jnp.int32, (rows, rows), 0)
    across = lax.broadcasted_iota(jnp.int32, (rows, rows), 1)
    return down, across


def features(index, width):
    return pl.ds(pl.multiple_of(index * width, width), width)


def fetch(pairs, sems):
    copies = [pltpu.make_async_copy(src, dst, sems.at[i]) for i, (src, dst) in enumerate(pairs)]
    for copy in copies:
        copy.start()
    return copies


def first_pack_kernel(place_ref, owner_ref, decay_hbm, key_hbm, value_hbm, *refs):
    decay_ref, key_ref, sems = refs[-3:]
    first = refs[:-3]
    count = len(first)
    rows, width = (first[0].shape[0] - TAIL) // 2, first[0].shape[1]
    place = place_ref[0] & (count - 1)
    pairs = [(decay_hbm, decay_ref), (key_hbm, key_ref)]
    for hop in range(count):
        pairs.append((value_hbm.at[:, features(2 * (place ^ hop), width)], first[hop].at[rows : 2 * rows]))
    copies = fetch(pairs, sems)
    down, across = iotas(rows)
    for copy in copies[:2]:
        copy.wait()
    for hop in range(count):
        head = place ^ hop
        decay = decay_ref[pl.ds(head, 1), :]
        after = jnp.sum(jnp.where(across > down, decay, 0.0), axis=1, keepdims=True)
        keys = key_ref[:, features(head, width)].astype(F32)
        first[hop][0:rows, :] = (keys * jnp.exp(after)).astype(BF16)
        whole = jnp.exp(jnp.sum(decay, axis=1, keepdims=True))
        whole = jnp.broadcast_to(whole, (TAIL, width))
        high = whole.astype(BF16).astype(F32)
        middle = (whole - high).astype(BF16).astype(F32)
        low = whole - high - middle
        row = lax.broadcasted_iota(jnp.int32, (TAIL, width), 0)
        tail = jnp.where(row == 0, high, jnp.where(row == 1, middle, jnp.where(row == 2, low, 0.0)))
        first[hop][2 * rows :, :] = tail.astype(BF16)
    for copy in copies[2:]:
        copy.wait()


def second_pack_kernel(place_ref, decay_hbm, query_hbm, value_hbm, *refs):
    decay_ref, query_ref, sems = refs[-3:]
    second = refs[:-3]
    count = len(second)
    rows, width = second[0].shape[0] // 2, second[0].shape[1]
    place = place_ref[0] & (count - 1)
    pairs = [(decay_hbm, decay_ref), (query_hbm, query_ref)]
    for hop in range(count):
        pairs.append((value_hbm.at[:, features(2 * (place ^ hop) + 1, width)], second[hop].at[0:rows]))
    copies = fetch(pairs, sems)
    down, across = iotas(rows)
    for copy in copies[:2]:
        copy.wait()
    for hop in range(count):
        head = place ^ hop
        decay = decay_ref[pl.ds(head, 1), :]
        upto = jnp.sum(jnp.where(across <= down, decay, 0.0), axis=1, keepdims=True)
        queries = query_ref[:, features(head, width)].astype(F32)
        second[hop][rows : 2 * rows, :] = (queries * jnp.exp(upto)).astype(BF16)
    for copy in copies[2:]:
        copy.wait()


def block_decay(message_ref):
    tail = message_ref[message_ref.shape[0] - TAIL :, :].astype(F32)
    return tail[0:1] + tail[1:2] + tail[2:3]


def outer(keys, values):
    return lax.dot_general(keys, values, (((0,), (0,)), ((), ())), preferred_element_type=F32)


def total_state(place, first, values, rows):
    decays = [block_decay(message) for message in first]
    total = None
    for hop, message in enumerate(first):
        scale = None
        for other in range(len(first)):
            if other != hop:
                factor = jnp.where((place ^ other) > (place ^ hop), decays[other], 1.0)
                scale = factor if scale is None else scale * factor
        term = outer(message[0:rows, :], values[hop])
        term = term if scale is None else term * scale
        total = term if total is None else total + term
    return total


def first_state_kernel(place_ref, *refs, rows):
    first, (state_ref, whole_ref) = refs[:-2], refs[-2:]
    values = [message[rows : 2 * rows, :] for message in first]
    state_ref[...] = total_state(place_ref[0] & (len(first) - 1), first, values, rows).astype(BF16)
    whole = block_decay(first[0])
    for message in first[1:]:
        whole = whole * block_decay(message)
    whole_ref[...] = jnp.broadcast_to(whole, whole_ref.shape)


def second_state_kernel(place_ref, token_ref, *refs, rows):
    count = (len(refs) - 1) // 2
    first, second, state_ref = refs[:count], refs[count : 2 * count], refs[-1]
    values = [message[0:rows, :] for message in second]
    state_ref[...] = total_state(place_ref[0] & (len(first) - 1), first, values, rows).astype(BF16)


def group_kernel(place_ref, *refs, rows):
    count = (len(refs) - 6) // 2
    first, second = refs[:count], refs[count : 2 * count]
    left_ref, right_ref, scaled_ref, states, earlier, decays = refs[2 * count :]
    width = first[0].shape[1]
    place = place_ref[0] & (count - 1)
    for hop in range(count):
        block = place ^ hop
        decays[block] = jnp.broadcast_to(block_decay(first[hop]), decays.shape[1:])
        keys = first[hop][0:rows, :]
        states[block, :, 0:width] = outer(keys, first[hop][rows : 2 * rows, :])
        states[block, :, width : 2 * width] = outer(keys, second[hop][0:rows, :])
    whole = jnp.ones((1, width), F32)
    for block in range(count):
        if block == 0:
            earlier[0] = jnp.zeros(earlier.shape[1:], BF16)
        elif block == 1:
            total = states[0]
            earlier[1] = total.astype(BF16)
        else:
            total = total * jnp.concatenate([decay, decay], axis=1) + states[block - 1]
            earlier[block] = total.astype(BF16)
        decay = decays[block][0:1]
        decays[block] = jnp.broadcast_to(whole, decays.shape[1:])
        whole = whole * decay
    for hop in range(count):
        block = place ^ hop
        queries = second[hop][rows : 2 * rows, :]
        here = slice(hop * rows, (hop + 1) * rows)
        part = jnp.dot(queries, earlier[block], preferred_element_type=F32)
        left_ref[here, :] = part[:, 0:width]
        right_ref[here, :] = part[:, width : 2 * width]
        scaled_ref[here, :] = (queries.astype(F32) * decays[block][0:1]).astype(BF16)


def cross_kernel(place_ref, state_ref, scaled_ref, part_ref, *out_refs):
    rows = out_refs[0].shape[0]
    carried = jnp.dot(scaled_ref[...], state_ref[...], preferred_element_type=F32)
    total = part_ref[...] + jnp.where(place_ref[0] < len(out_refs), 0.0, carried)
    for hop, out_ref in enumerate(out_refs):
        out_ref[...] = total[hop * rows : (hop + 1) * rows, :].astype(BF16)


def block_kernel(*refs):
    _, decay_hbm, query_hbm, key_hbm, value_hbm, gate_hbm, inner_ref, swish_ref, token_ref = refs[:9]
    decay_ref, query_ref, key_ref, value_ref, gate_ref, sems = refs[9:]
    rows = query_ref.shape[0]
    heads = decay_ref.shape[0]
    key_dim, value_dim = query_ref.shape[1] // heads, value_ref.shape[1] // heads
    copies = fetch(
        [
            (decay_hbm, decay_ref),
            (query_hbm, query_ref),
            (key_hbm, key_ref),
            (value_hbm, value_ref),
            (gate_hbm, gate_ref),
        ],
        sems,
    )
    down, across = iotas(rows)
    causal = across <= down
    for copy in copies:
        copy.wait()
    for head in range(heads):
        decay = decay_ref[head : head + 1, :]
        column = jnp.sum(jnp.where(causal, decay, 0.0), axis=1, keepdims=True)
        line = jnp.sum(jnp.where(across == down, column, 0.0), axis=0, keepdims=True)
        table = jnp.where(causal, jnp.exp(jnp.where(causal, column - line, 0.0)), 0.0)
        keys = slice(head * key_dim, (head + 1) * key_dim)
        here = slice(head * value_dim, (head + 1) * value_dim)
        scores = lax.dot_general(
            query_ref[:, keys], key_ref[:, keys], (((1,), (1,)), ((), ())), preferred_element_type=F32
        )
        inner_ref[:, here] = jnp.dot(
            (scores * table).astype(BF16), value_ref[:, here], preferred_element_type=F32
        )
        gate = gate_ref[:, here].astype(F32)
        swish_ref[:, here] = gate / (1.0 + jnp.exp(-gate))
    token_ref[...] = jnp.zeros_like(token_ref)


def mix(place_ref, owner_ref, inner_ref, swish_ref, part_refs, mixed, hop, group, owners):
    rows, value_dim = mixed.shape
    here = features((place_ref[0] & (group - 1)) ^ hop, value_dim)
    part = jnp.concatenate([part_ref[...] for part_ref in part_refs], axis=1)
    retained = inner_ref[:, here] + part.astype(F32)
    mean = jnp.mean(retained, axis=1, keepdims=True)
    centered = retained - mean
    variance = jnp.mean(centered * centered, axis=1, keepdims=True)
    mixed[...] = centered * lax.rsqrt(variance + 1e-05) * swish_ref[:, here]
    share = rows // owners
    bits = owners.bit_length() - 1
    pieces = []
    for position in range(owners):
        flipped = owners - 1 - position
        mask = sum(((flipped >> bit) & 1) << (bits - 1 - bit) for bit in range(bits))
        start = pl.multiple_of((owner_ref[0] ^ mask) * share, share)
        pieces.append(mixed[pl.ds(start, share), :])
    return jnp.concatenate(pieces, axis=0).astype(BF16)


def head_product(place_ref, rows, weight_ref, hop, group, start, tile):
    depth = rows.shape[1]
    return jnp.dot(
        rows,
        weight_ref[features((place_ref[0] & (group - 1)) ^ hop, depth), start : start + tile],
        preferred_element_type=F32,
    )


def add_head_kernel(*refs, hop, group, owners):
    place_ref, owner_ref, inner_ref, swish_ref, weight_ref = refs[:5]
    before, part_refs = refs[5 : 5 + (hop > 0)], refs[5 + (hop > 0) : -2]
    total_ref, mixed = refs[-2:]
    rows = mix(place_ref, owner_ref, inner_ref, swish_ref, part_refs, mixed, hop, group, owners)
    width = total_ref.shape[1]
    tile = min(512, width)
    for start in range(0, width, tile):
        here = slice(start, start + tile)
        term = head_product(place_ref, rows, weight_ref, hop, group, start, tile)
        total_ref[:, here] = before[0][:, here] + term if before else term


def finish_part(place_ref, rows, weight_ref, totals, send_ref, keep_ref, offset, late, group):
    half, width = send_ref.shape
    tile = min(512, width)
    for start in range(0, width, tile):
        here = slice(start, start + tile)
        there = offset + start
        terms = [
            head_product(place_ref, rows_ref[...], weight_ref, hop, group, there, tile)
            for hop, rows_ref in zip(late, rows)
        ]
        terms += [total_ref[:, there : there + tile] for total_ref in totals]
        out = functools.reduce(jnp.add, terms)
        send_ref[:, here] = out[:half].astype(BF16)
        keep_ref[:, here] = out[half:].astype(BF16)


def first_part_kernel(*refs, late, group, owners):
    place_ref, owner_ref, inner_ref, swish_ref, weight_ref = refs[:5]
    count = len(late)
    totals, part_refs = refs[5 : 5 + (late[0] > 0)], refs[5 + (late[0] > 0) : -3 - count]
    send_ref, keep_ref, mixed = refs[-3 - count], refs[-2 - count], refs[-1]
    rows = refs[-1 - count : -1]
    each = len(part_refs) // count
    for at, (hop, rows_ref) in enumerate(zip(late, rows)):
        mine = part_refs[at * each : (at + 1) * each]
        rows_ref[...] = mix(place_ref, owner_ref, inner_ref, swish_ref, mine, mixed, hop, group, owners)
    finish_part(place_ref, rows, weight_ref, totals, send_ref, keep_ref, 0, late, group)


def other_part_kernel(place_ref, weight_ref, *refs, offset, late, group):
    count = len(late)
    send_ref, keep_ref = refs[-2:]
    finish_part(place_ref, refs[:count], weight_ref, refs[count:-2], send_ref, keep_ref, offset, late, group)


def swap(value, axis, size, mask):
    return lax.ppermute(value, axis, [(i, i ^ mask) for i in range(size)])


def swaps(values, axis, size):
    return [swap(values[hop], axis, size, hop) for hop in range(1, len(values))]


def carried_into(state, whole, axis, size, group):
    def shift(value, by):
        return lax.ppermute(value, axis, [(i, (i + by * group) % size) for i in range(size)])

    groups = size // group
    if groups == 1:
        return state
    got = shift(state, 1)
    if groups == 2:
        return got
    first = lax.axis_index(axis) < group
    total, product = jnp.where(first, 0.0, got.astype(F32)), jnp.where(first, 1.0, shift(whole, 1))
    by = 1
    while by < groups - 1:
        none = lax.axis_index(axis) < by * group
        earlier, before = shift(total.astype(BF16), by), shift(product, by)
        total = total + jnp.where(none, 0.0, product[0:1] * earlier.astype(F32))
        product = product * jnp.where(none, 1.0, before)
        by *= 2
    return total.astype(BF16)


def reduce_over(send, keep, axis, size):
    keep = keep.astype(F32)
    mask = 1
    while mask < size:
        keep = keep + swap(send.astype(BF16), axis, size, mask).astype(F32)
        mask *= 2
        if mask < size:
            half = keep.shape[0] // 2
            send, keep = keep[:half], keep[half:]
    return keep.astype(BF16)


def local(query, key, value, gate, decay, weight, *, ctx, head):
    rows = query.shape[0]
    heads = decay.shape[0]
    key_dim = query.shape[1] // heads
    value_dim = value.shape[1] // heads
    depth, width = weight.shape
    group = heads
    me = lax.axis_index("ctx")
    place = me.astype(jnp.int32).reshape(1)
    owner = lax.axis_index("head").astype(jnp.int32).reshape(1)
    shape = jax.ShapeDtypeStruct

    def after(value):
        return lax.optimization_barrier((decay, value))[0]

    first = pl.pallas_call(
        first_pack_kernel,
        out_shape=[shape((2 * rows + TAIL, key_dim), BF16)] * group,
        in_specs=[SMEM] * 2 + [HBM] * 3,
        out_specs=[VMEM] * group,
        scratch_shapes=[
            pltpu.VMEM(decay.shape, F32),
            pltpu.VMEM(key.shape, BF16),
            pltpu.SemaphoreType.DMA((2 + group,)),
        ],
        compiler_params=params(8),
        cost_estimate=cost(5 * 10**9, 2**24),
        name="first_pack",
    )(place, owner, *in_hbm(decay, key, value))
    second = pl.pallas_call(
        second_pack_kernel,
        out_shape=[shape((2 * rows, key_dim), BF16)] * group,
        in_specs=[SMEM] + [HBM] * 3,
        out_specs=[VMEM] * group,
        scratch_shapes=[
            pltpu.VMEM(decay.shape, F32),
            pltpu.VMEM(query.shape, BF16),
            pltpu.SemaphoreType.DMA((2 + group,)),
        ],
        compiler_params=params(8),
        name="second_pack",
    )(place, *in_hbm(after(first[0]), query, value))
    first = [first[0]] + swaps(first, "ctx", ctx)
    second = [second[0]] + swaps(second, "ctx", ctx)
    left_state, whole = pl.pallas_call(
        functools.partial(first_state_kernel, rows=rows),
        out_shape=[shape((key_dim, key_dim), BF16), shape((8, key_dim), F32)],
        in_specs=[SMEM] + [VMEM] * group,
        out_specs=[VMEM] * 2,
        compiler_params=params(8),
        cost_estimate=cost(5*10**9, 2**24),
        name="first_state",
    )(place, *first)
    left_carried = carried_into(left_state, whole, "ctx", ctx, group)

    inner, swish, token = pl.pallas_call(
        block_kernel,
        out_shape=[shape(value.shape, F32)] * 2 + [shape((8, 128), F32)],
        in_specs=[VMEM] + [HBM] * 5,
        out_specs=[VMEM] * 3,
        scratch_shapes=[
            pltpu.VMEM(decay.shape, F32),
            pltpu.VMEM(query.shape, BF16),
            pltpu.VMEM(key.shape, BF16),
            pltpu.VMEM(value.shape, BF16),
            pltpu.VMEM(gate.shape, BF16),
            pltpu.SemaphoreType.DMA((5,)),
        ],
        compiler_params=params(8),
        cost_estimate=cost(10**9, 4 * 2**20),
        name="block_part",
    )(whole, *in_hbm(decay, query, key, value, gate))

    right_state = pl.pallas_call(
        functools.partial(second_state_kernel, rows=rows),
        out_shape=shape((key_dim, key_dim), BF16),
        in_specs=[SMEM] + [VMEM] * (1 + 2 * group),
        out_specs=VMEM,
        compiler_params=params(8),
        cost_estimate=cost(5*10**9, 2**24),
        name="second_state",
    )(place, token, *first, *second)
    right_carried = carried_into(right_state, whole, "ctx", ctx, group)

    left_part, right_part, scaled = pl.pallas_call(
        functools.partial(group_kernel, rows=rows),
        out_shape=[shape((group * rows, key_dim), F32)] * 2 + [shape((group * rows, key_dim), BF16)],
        in_specs=[SMEM] + [VMEM] * (2 * group),
        out_specs=[VMEM] * 3,
        scratch_shapes=[
            pltpu.VMEM((group, key_dim, value_dim), F32),
            pltpu.VMEM((group, key_dim, value_dim), BF16),
            pltpu.VMEM((group, 8, key_dim), F32),
        ],
        compiler_params=params(8),
        cost_estimate=cost(10**9, 4 * 2**20),
        name="group_part",
    )(place, *first, *second)

    def cross(carried, part, name):
        parts = pl.pallas_call(
            cross_kernel,
            out_shape=[shape((rows, key_dim), BF16)] * group,
            in_specs=[SMEM] + [VMEM] * 3,
            out_specs=[VMEM] * group,
            compiler_params=params(8),
            name=name,
        )(place, carried, scaled, part)
        return [parts[0]] + swaps(parts, "ctx", ctx)

    left_parts = cross(left_carried, left_part, "left_cross")
    right_parts = cross(right_carried, right_part, "right_cross")
    inner, left_parts = lax.optimization_barrier((inner, left_parts))
    parts = list(zip(left_parts, right_parts))
    late = list(range(group))[-1:]
    total = []
    for hop in range(late[0]):
        total = [
            pl.pallas_call(
                functools.partial(add_head_kernel, hop=hop, group=group, owners=head),
                out_shape=shape((rows, width), F32),
                in_specs=[SMEM] * 2 + [VMEM] * (3 + len(total) + len(parts[hop])),
                out_specs=VMEM,
                input_output_aliases={5: 0} if total else {},
                scratch_shapes=[pltpu.VMEM((rows, value_dim), F32)],
                compiler_params=params(4),
                name="add_head",
            )(place, owner, inner, swish, weight, *total, *parts[hop])
        ]
    late_parts = [piece for hop in late for piece in parts[hop]]
    outs = []
    offset = 0
    for part, columns in enumerate((width * 3 // 8, width * 5 // 8)):
        halves = [shape((rows // 2, columns), BF16)] * 2
        if part == 0:
            send, keep, *last_rows = pl.pallas_call(
                functools.partial(first_part_kernel, late=late, group=group, owners=head),
                out_shape=halves + [shape((rows, value_dim), BF16)] * len(late),
                in_specs=[SMEM] * 2 + [VMEM] * (3 + len(total) + len(late_parts)),
                out_specs=[VMEM] * (2 + len(late)),
                scratch_shapes=[pltpu.VMEM((rows, value_dim), F32)],
                compiler_params=params(4),
                name="first_part",
            )(place, owner, inner, swish, weight, *total, *late_parts)
        else:
            send, keep = pl.pallas_call(
                functools.partial(other_part_kernel, offset=offset, late=late, group=group),
                out_shape=halves,
                in_specs=[SMEM] + [VMEM] * (1 + len(late) + len(total)),
                out_specs=[VMEM] * 2,
                compiler_params=params(4),
                name="other_part",
            )(place, weight, *last_rows, *total)
        outs.append(reduce_over(send, keep, "head", head))
        offset += columns
    return jnp.concatenate(outs, axis=1)


def solution(mesh):
    in_specs = (
        P("ctx", "head"),
        P("ctx", "head"),
        P("ctx", "head"),
        P("ctx", "head"),
        P("head", "ctx"),
        P("head", None),
    )
    out_specs = P(("ctx", "head"), None)
    body = functools.partial(local, ctx=mesh.shape["ctx"], head=mesh.shape["head"])
    return jax.shard_map(body, mesh=mesh, in_specs=in_specs, out_specs=out_specs, check_vma=False)
```

```python
import functools
import jax
import jax.numpy as jnp
from jax import lax
from jax.experimental import pallas as pl
from jax.experimental.pallas import tpu as pltpu
from jax.sharding import PartitionSpec as P

F32 = jnp.float32
BF16 = jnp.bfloat16
TAIL = 16
SMEM = pl.BlockSpec(memory_space=pltpu.SMEM)
VMEM = pl.BlockSpec(memory_space=pltpu.VMEM)
HBM = pl.BlockSpec(memory_space=pltpu.HBM)


def params(mib):
    return pltpu.CompilerParams(vmem_limit_bytes=mib * 2**20)


def cost(flops, bytes_accessed):
    return pl.CostEstimate(flops=flops, bytes_accessed=bytes_accessed, transcendentals=0)


def in_hbm(*values):
    return [pltpu.with_memory_space_constraint(value, pltpu.HBM) for value in values]


def iotas(rows):
    down = lax.broadcasted_iota(jnp.int32, (rows, rows), 0)
    across = lax.broadcasted_iota(jnp.int32, (rows, rows), 1)
    return down, across


def features(index, width):
    return pl.ds(pl.multiple_of(index * width, width), width)


def by_owner(scratch, value, owner, owners):
    scratch[...] = value
    share = value.shape[0] // owners
    bits = owners.bit_length() - 1
    pieces = []
    for position in range(owners):
        flipped = owners - 1 - position
        mask = sum(((flipped >> bit) & 1) << (bits - 1 - bit) for bit in range(bits))
        pieces.append(scratch[pl.ds(pl.multiple_of((owner ^ mask) * share, share), share), :])
    return jnp.concatenate(pieces, axis=0)


def fetch(pairs, sems):
    copies = [pltpu.make_async_copy(src, dst, sems.at[i]) for i, (src, dst) in enumerate(pairs)]
    for copy in copies:
        copy.start()
    return copies


def first_pack_kernel(place_ref, owner_ref, decay_hbm, key_hbm, value_hbm, *refs):
    decay_ref, key_ref, sems = refs[-3:]
    first = refs[:-3]
    count = len(first)
    rows, width = (first[0].shape[0] - TAIL) // 2, first[0].shape[1]
    place = place_ref[0] & (count - 1)
    pairs = [(decay_hbm, decay_ref), (key_hbm, key_ref)]
    for hop in range(count):
        pairs.append((value_hbm.at[:, features(2 * (place ^ hop), width)], first[hop].at[rows : 2 * rows]))
    copies = fetch(pairs, sems)
    down, across = iotas(rows)
    copies[0].wait()
    scales = []
    for hop in range(count):
        decay = decay_ref[pl.ds(place ^ hop, 1), :]
        after = jnp.sum(jnp.where(across > down, decay, 0.0), axis=1, keepdims=True)
        scales.append(jnp.exp(after))
        whole = jnp.exp(jnp.sum(decay, axis=1, keepdims=True))
        whole = jnp.broadcast_to(whole, (TAIL, width))
        high = whole.astype(BF16).astype(F32)
        middle = (whole - high).astype(BF16).astype(F32)
        low = whole - high - middle
        row = lax.broadcasted_iota(jnp.int32, (TAIL, width), 0)
        tail = jnp.where(row == 0, high, jnp.where(row == 1, middle, jnp.where(row == 2, low, 0.0)))
        first[hop][2 * rows :, :] = tail.astype(BF16)
    copies[1].wait()
    for hop in range(count):
        keys = key_ref[:, features(place ^ hop, width)].astype(F32)
        first[hop][0:rows, :] = (keys * scales[hop]).astype(BF16)
    for copy in copies[2:]:
        copy.wait()


def second_pack_kernel(place_ref, owner_ref, decay_hbm, query_hbm, value_hbm, *refs, owners):
    decay_ref, query_ref, ordered, sems = refs[-4:]
    second = refs[:-4]
    count = len(second)
    rows, width = second[0].shape[0] // 2, second[0].shape[1]
    place = place_ref[0] & (count - 1)
    pairs = [(decay_hbm, decay_ref), (query_hbm, query_ref)]
    for hop in range(count):
        pairs.append((value_hbm.at[:, features(2 * (place ^ hop) + 1, width)], second[hop].at[0:rows]))
    copies = fetch(pairs, sems)
    down, across = iotas(rows)
    for copy in copies[:2]:
        copy.wait()
    for hop in range(count):
        head = place ^ hop
        decay = decay_ref[pl.ds(head, 1), :]
        upto = jnp.sum(jnp.where(across <= down, decay, 0.0), axis=1, keepdims=True)
        queries = query_ref[:, features(head, width)].astype(F32)
        queries = by_owner(ordered, queries * jnp.exp(upto), owner_ref[0], owners)
        second[hop][rows : 2 * rows, :] = queries.astype(BF16)
    for copy in copies[2:]:
        copy.wait()


def block_decay(message_ref):
    tail = message_ref[message_ref.shape[0] - TAIL :, :].astype(F32)
    return tail[0:1] + tail[1:2] + tail[2:3]


def outer(keys, values):
    return lax.dot_general(keys, values, (((0,), (0,)), ((), ())), preferred_element_type=F32)


def total_state(place, first, values, rows):
    decays = [block_decay(message) for message in first]
    total = None
    for hop, message in enumerate(first):
        scale = None
        for other in range(len(first)):
            if other != hop:
                factor = jnp.where((place ^ other) > (place ^ hop), decays[other], 1.0)
                scale = factor if scale is None else scale * factor
        term = outer(message[0:rows, :], values[hop])
        term = term if scale is None else term * scale
        total = term if total is None else total + term
    return total


def first_state_kernel(place_ref, *refs, rows):
    first, (state_ref, whole_ref) = refs[:-2], refs[-2:]
    values = [message[rows : 2 * rows, :] for message in first]
    state_ref[...] = total_state(place_ref[0] & (len(first) - 1), first, values, rows).astype(BF16)
    whole = block_decay(first[0])
    for message in first[1:]:
        whole = whole * block_decay(message)
    whole_ref[...] = jnp.broadcast_to(whole, whole_ref.shape)


def second_state_kernel(place_ref, token_ref, *refs, rows):
    count = (len(refs) - 1) // 2
    first, second, state_ref = refs[:count], refs[count : 2 * count], refs[-1]
    values = [message[0:rows, :] for message in second]
    state_ref[...] = total_state(place_ref[0] & (len(first) - 1), first, values, rows).astype(BF16)


def group_kernel(place_ref, *refs, rows):
    count = (len(refs) - 6) // 2
    first, second = refs[:count], refs[count : 2 * count]
    left_ref, right_ref, scaled_ref, states, earlier, decays = refs[2 * count :]
    width = first[0].shape[1]
    place = place_ref[0] & (count - 1)
    for hop in range(count):
        block = place ^ hop
        decays[block] = jnp.broadcast_to(block_decay(first[hop]), decays.shape[1:])
        keys = first[hop][0:rows, :]
        states[block, :, 0:width] = outer(keys, first[hop][rows : 2 * rows, :])
        states[block, :, width : 2 * width] = outer(keys, second[hop][0:rows, :])
    whole = jnp.ones((1, width), F32)
    for block in range(count):
        if block == 0:
            earlier[0] = jnp.zeros(earlier.shape[1:], BF16)
        elif block == 1:
            total = states[0]
            earlier[1] = total.astype(BF16)
        else:
            total = total * jnp.concatenate([decay, decay], axis=1) + states[block - 1]
            earlier[block] = total.astype(BF16)
        decay = decays[block][0:1]
        decays[block] = jnp.broadcast_to(whole, decays.shape[1:])
        whole = whole * decay
    for hop in range(count):
        block = place ^ hop
        queries = second[hop][rows : 2 * rows, :]
        here = slice(hop * rows, (hop + 1) * rows)
        part = jnp.dot(queries, earlier[block], preferred_element_type=F32)
        left_ref[here, :] = part[:, 0:width]
        right_ref[here, :] = part[:, width : 2 * width]
        scaled_ref[here, :] = (queries.astype(F32) * decays[block][0:1]).astype(BF16)


def cross_kernel(place_ref, state_ref, scaled_ref, part_ref, *out_refs):
    rows = out_refs[0].shape[0]
    carried = jnp.dot(scaled_ref[...], state_ref[...], preferred_element_type=F32)
    total = part_ref[...] + jnp.where(place_ref[0] < len(out_refs), 0.0, carried)
    for hop, out_ref in enumerate(out_refs):
        out_ref[...] = total[hop * rows : (hop + 1) * rows, :].astype(BF16)


def block_kernel(owner_ref, *refs, owners):
    _, decay_hbm, query_hbm, key_hbm, value_hbm, gate_hbm, inner_ref, swish_ref, token_ref = refs[:9]
    decay_ref, query_ref, key_ref, value_ref, gate_ref, ordered, sems = refs[9:]
    rows = query_ref.shape[0]
    heads = decay_ref.shape[0]
    key_dim, value_dim = query_ref.shape[1] // heads, value_ref.shape[1] // heads
    copies = fetch(
        [
            (decay_hbm, decay_ref),
            (query_hbm, query_ref),
            (key_hbm, key_ref),
            (value_hbm, value_ref),
            (gate_hbm, gate_ref),
        ],
        sems,
    )
    down, across = iotas(rows)
    causal = across <= down
    for copy in copies:
        copy.wait()
    for head in range(heads):
        decay = decay_ref[head : head + 1, :]
        column = jnp.sum(jnp.where(causal, decay, 0.0), axis=1, keepdims=True)
        line = jnp.sum(jnp.where(across == down, column, 0.0), axis=0, keepdims=True)
        table = jnp.where(causal, jnp.exp(jnp.where(causal, column - line, 0.0)), 0.0)
        keys = slice(head * key_dim, (head + 1) * key_dim)
        here = slice(head * value_dim, (head + 1) * value_dim)
        scores = lax.dot_general(
            query_ref[:, keys], key_ref[:, keys], (((1,), (1,)), ((), ())), preferred_element_type=F32
        )
        inner = jnp.dot((scores * table).astype(BF16), value_ref[:, here], preferred_element_type=F32)
        inner_ref[:, here] = by_owner(ordered.at[0], inner, owner_ref[0], owners)
        gate = gate_ref[:, here].astype(F32)
        swish_ref[:, here] = by_owner(ordered.at[1], gate / (1.0 + jnp.exp(-gate)), owner_ref[0], owners)
    token_ref[...] = jnp.zeros_like(token_ref)


def mix(place_ref, inner_ref, swish_ref, part_refs, hop, group):
    value_dim = sum(part_ref.shape[1] for part_ref in part_refs)
    here = features((place_ref[0] & (group - 1)) ^ hop, value_dim)
    part = jnp.concatenate([part_ref[...] for part_ref in part_refs], axis=1)
    retained = inner_ref[:, here] + part.astype(F32)
    mean = jnp.mean(retained, axis=1, keepdims=True)
    centered = retained - mean
    variance = jnp.mean(centered * centered, axis=1, keepdims=True)
    return centered * lax.rsqrt(variance + 1e-05) * swish_ref[:, here]


def head_product(place_ref, rows, weight_ref, hop, group, start, tile):
    depth = rows.shape[1]
    return jnp.dot(
        rows,
        weight_ref[features((place_ref[0] & (group - 1)) ^ hop, depth), start : start + tile],
        preferred_element_type=F32,
    )


def add_head_kernel(*refs, hop, group, summed):
    place_ref, inner_ref, swish_ref, weight_ref = refs[:4]
    before, part_refs = refs[4 : 4 + summed], refs[4 + summed : -2]
    total_ref, mixed = refs[-2:]
    mixed[...] = mix(place_ref, inner_ref, swish_ref, part_refs, hop, group)
    rows = mixed[...].astype(BF16)
    width = total_ref.shape[1]
    tile = min(512, width)
    for start in range(0, width, tile):
        here = slice(start, start + tile)
        term = head_product(place_ref, rows, weight_ref, hop, group, start, tile)
        total_ref[:, here] = before[0][:, here] + term if before else term


def finish_part(place_ref, rows, weight_ref, totals, send_ref, keep_ref, offset, late, group):
    half, width = send_ref.shape
    tile = min(512, width)
    for start in range(0, width, tile):
        here = slice(start, start + tile)
        there = offset + start
        terms = [
            head_product(place_ref, rows_ref[...], weight_ref, hop, group, there, tile)
            for hop, rows_ref in zip(late, rows)
        ]
        terms += [total_ref[:, there : there + tile] for total_ref in totals]
        out = functools.reduce(jnp.add, terms)
        send_ref[:, here] = out[:half].astype(BF16)
        keep_ref[:, here] = out[half:].astype(BF16)


def first_part_kernel(*refs, late, group, summed):
    place_ref, inner_ref, swish_ref, weight_ref = refs[:4]
    count = len(late)
    totals, part_refs = refs[4 : 4 + summed], refs[4 + summed : -2 - count]
    send_ref, keep_ref = refs[-2 - count], refs[-1 - count]
    rows = refs[-count:]
    each = len(part_refs) // count
    for at, (hop, rows_ref) in enumerate(zip(late, rows)):
        rows_ref[...] = mix(place_ref, inner_ref, swish_ref, part_refs[at * each : (at + 1) * each], hop, group).astype(BF16)
    finish_part(place_ref, rows, weight_ref, totals, send_ref, keep_ref, 0, late, group)


def other_part_kernel(place_ref, weight_ref, *refs, offset, late, group):
    count = len(late)
    send_ref, keep_ref = refs[-2:]
    finish_part(place_ref, refs[:count], weight_ref, refs[count:-2], send_ref, keep_ref, offset, late, group)


def swap(value, axis, size, mask):
    return lax.ppermute(value, axis, [(i, i ^ mask) for i in range(size)])


def swaps(values, axis, size):
    return [swap(values[hop], axis, size, hop) for hop in range(1, len(values))]


def carried_into(state, whole, axis, size, group):
    def shift(value, by):
        return lax.ppermute(value, axis, [(i, (i + by * group) % size) for i in range(size)])

    groups = size // group
    if groups == 1:
        return state
    got = shift(state, 1)
    if groups == 2:
        return got
    first = lax.axis_index(axis) < group
    total, product = jnp.where(first, 0.0, got.astype(F32)), jnp.where(first, 1.0, shift(whole, 1))
    by = 1
    while by < groups - 1:
        none = lax.axis_index(axis) < by * group
        earlier, before = shift(total.astype(BF16), by), shift(product, by)
        total = total + jnp.where(none, 0.0, product[0:1] * earlier.astype(F32))
        product = product * jnp.where(none, 1.0, before)
        by *= 2
    return total.astype(BF16)


def reduce_over(send, keep, axis, size):
    keep = keep.astype(F32)
    mask = 1
    while mask < size:
        keep = keep + swap(send.astype(BF16), axis, size, mask).astype(F32)
        mask *= 2
        if mask < size:
            half = keep.shape[0] // 2
            send, keep = keep[:half], keep[half:]
    return keep.astype(BF16)


def local(query, key, value, gate, decay, weight, *, ctx, head):
    rows = query.shape[0]
    heads = decay.shape[0]
    key_dim = query.shape[1] // heads
    value_dim = value.shape[1] // heads
    depth, width = weight.shape
    group = heads
    me = lax.axis_index("ctx")
    place = me.astype(jnp.int32).reshape(1)
    owner = lax.axis_index("head").astype(jnp.int32).reshape(1)
    shape = jax.ShapeDtypeStruct

    def after(value):
        return lax.optimization_barrier((decay, value))[0]

    first = pl.pallas_call(
        first_pack_kernel,
        out_shape=[shape((2 * rows + TAIL, key_dim), BF16)] * group,
        in_specs=[SMEM] * 2 + [HBM] * 3,
        out_specs=[VMEM] * group,
        scratch_shapes=[
            pltpu.VMEM(decay.shape, F32),
            pltpu.VMEM(key.shape, BF16),
            pltpu.SemaphoreType.DMA((2 + group,)),
        ],
        compiler_params=params(8),
        cost_estimate=cost(5 * 10**9, 2**24),
        name="first_pack",
    )(place, owner, *in_hbm(decay, key, value))
    second = pl.pallas_call(
        functools.partial(second_pack_kernel, owners=head),
        out_shape=[shape((2 * rows, key_dim), BF16)] * group,
        in_specs=[SMEM] * 2 + [HBM] * 3,
        out_specs=[VMEM] * group,
        scratch_shapes=[
            pltpu.VMEM(decay.shape, F32),
            pltpu.VMEM(query.shape, BF16),
            pltpu.VMEM((rows, key_dim), F32),
            pltpu.SemaphoreType.DMA((2 + group,)),
        ],
        compiler_params=params(8),
        name="second_pack",
    )(place, owner, *in_hbm(after(first[0]), query, value))
    first = [first[0]] + swaps(first, "ctx", ctx)
    second = [second[0]] + swaps(second, "ctx", ctx)
    left_state, whole = pl.pallas_call(
        functools.partial(first_state_kernel, rows=rows),
        out_shape=[shape((key_dim, key_dim), BF16), shape((8, key_dim), F32)],
        in_specs=[SMEM] + [VMEM] * group,
        out_specs=[VMEM] * 2,
        compiler_params=params(8),
        cost_estimate=cost(5*10**9, 2**24),
        name="first_state",
    )(place, *first)
    left_carried = carried_into(left_state, whole, "ctx", ctx, group)

    inner, swish, token = pl.pallas_call(
        functools.partial(block_kernel, owners=head),
        out_shape=[shape(value.shape, F32)] * 2 + [shape((8, 128), F32)],
        in_specs=[SMEM, VMEM] + [HBM] * 5,
        out_specs=[VMEM] * 3,
        scratch_shapes=[
            pltpu.VMEM(decay.shape, F32),
            pltpu.VMEM(query.shape, BF16),
            pltpu.VMEM(key.shape, BF16),
            pltpu.VMEM(value.shape, BF16),
            pltpu.VMEM(gate.shape, BF16),
            pltpu.VMEM((2, rows, value_dim), F32),
            pltpu.SemaphoreType.DMA((5,)),
        ],
        compiler_params=params(8),
        cost_estimate=cost(10**9, 4 * 2**20),
        name="block_part",
    )(owner, whole, *in_hbm(decay, query, key, value, gate))

    right_state = pl.pallas_call(
        functools.partial(second_state_kernel, rows=rows),
        out_shape=shape((key_dim, key_dim), BF16),
        in_specs=[SMEM] + [VMEM] * (1 + 2 * group),
        out_specs=VMEM,
        compiler_params=params(8),
        cost_estimate=cost(5*10**9, 2**24),
        name="second_state",
    )(place, token, *first, *second)
    right_carried = carried_into(right_state, whole, "ctx", ctx, group)

    left_part, right_part, scaled = pl.pallas_call(
        functools.partial(group_kernel, rows=rows),
        out_shape=[shape((group * rows, key_dim), F32)] * 2 + [shape((group * rows, key_dim), BF16)],
        in_specs=[SMEM] + [VMEM] * (2 * group),
        out_specs=[VMEM] * 3,
        scratch_shapes=[
            pltpu.VMEM((group, key_dim, value_dim), F32),
            pltpu.VMEM((group, key_dim, value_dim), BF16),
            pltpu.VMEM((group, 8, key_dim), F32),
        ],
        compiler_params=params(8),
        cost_estimate=cost(10**9, 4 * 2**20),
        name="group_part",
    )(place, *first, *second)

    def cross(carried, part, name):
        parts = pl.pallas_call(
            cross_kernel,
            out_shape=[shape((rows, key_dim), BF16)] * group,
            in_specs=[SMEM] + [VMEM] * 3,
            out_specs=[VMEM] * group,
            compiler_params=params(8),
            name=name,
        )(place, carried, scaled, part)
        return [parts[0]] + swaps(parts, "ctx", ctx)

    left_parts = cross(left_carried, left_part, "left_cross")
    right_parts = cross(right_carried, right_part, "right_cross")
    inner, left_parts = lax.optimization_barrier((inner, left_parts))
    parts = list(zip(left_parts, right_parts))
    hops = [0, *range(2, group), *range(1, min(2, group))]
    late = hops[-1:]
    total = []
    for hop in hops[:-1]:
        total = [
            pl.pallas_call(
                functools.partial(add_head_kernel, hop=hop, group=group, summed=len(total)),
                out_shape=shape((rows, width), F32),
                in_specs=[SMEM] + [VMEM] * (3 + len(total) + len(parts[hop])),
                out_specs=VMEM,

                scratch_shapes=[pltpu.VMEM((rows, value_dim), F32)],
                compiler_params=params(4),
                name="add_head",
            )(place, inner, swish, weight, *total, *parts[hop])
        ]
    late_parts = [piece for hop in late for piece in parts[hop]]
    outs = []
    offset = 0
    for part, columns in enumerate((width * 3 // 8, width * 5 // 8)):
        halves = [shape((rows // 2, columns), BF16)] * 2
        if part == 0:
            send, keep, *last_rows = pl.pallas_call(
                functools.partial(first_part_kernel, late=late, group=group, summed=len(total)),
                out_shape=halves + [shape((rows, value_dim), BF16)] * len(late),
                in_specs=[SMEM] + [VMEM] * (3 + len(total) + len(late_parts)),
                out_specs=[VMEM] * (2 + len(late)),
                compiler_params=params(4),
                name="first_part",
            )(place, inner, swish, weight, *total, *late_parts)
        else:
            send, keep = pl.pallas_call(
                functools.partial(other_part_kernel, offset=offset, late=late, group=group),
                out_shape=halves,
                in_specs=[SMEM] + [VMEM] * (1 + len(late) + len(total)),
                out_specs=[VMEM] * 2,
                compiler_params=params(4),
                name="other_part",
            )(place, weight, *last_rows, *total)
        outs.append(reduce_over(send, keep, "head", head))
        offset += columns
    return jnp.concatenate(outs, axis=1)


def solution(mesh):
    in_specs = (
        P("ctx", "head"),
        P("ctx", "head"),
        P("ctx", "head"),
        P("ctx", "head"),
        P("head", "ctx"),
        P("head", None),
    )
    out_specs = P(("ctx", "head"), None)
    body = functools.partial(local, ctx=mesh.shape["ctx"], head=mesh.shape["head"])
    return jax.shard_map(body, mesh=mesh, in_specs=in_specs, out_specs=out_specs, check_vma=False)
```

```python
import functools
import jax
import jax.numpy as jnp
from jax import lax
from jax.experimental import pallas as pl
from jax.experimental.pallas import tpu as pltpu
from jax.sharding import PartitionSpec as P

F32 = jnp.float32
BF16 = jnp.bfloat16
TAIL = 16
SMEM = pl.BlockSpec(memory_space=pltpu.SMEM)
VMEM = pl.BlockSpec(memory_space=pltpu.VMEM)
HBM = pl.BlockSpec(memory_space=pltpu.HBM)


def params(mib):
    return pltpu.CompilerParams(vmem_limit_bytes=mib * 2**20)


def cost(flops, bytes_accessed):
    return pl.CostEstimate(flops=flops, bytes_accessed=bytes_accessed, transcendentals=0)


def in_hbm(*values):
    return [pltpu.with_memory_space_constraint(value, pltpu.HBM) for value in values]


def iotas(rows):
    down = lax.broadcasted_iota(jnp.int32, (rows, rows), 0)
    across = lax.broadcasted_iota(jnp.int32, (rows, rows), 1)
    return down, across


def features(index, width):
    return pl.ds(pl.multiple_of(index * width, width), width)


def by_owner(scratch, value, owner, owners):
    scratch[...] = value
    share = value.shape[0] // owners
    bits = owners.bit_length() - 1
    pieces = []
    for position in range(owners):
        flipped = owners - 1 - position
        mask = sum(((flipped >> bit) & 1) << (bits - 1 - bit) for bit in range(bits))
        pieces.append(scratch[pl.ds(pl.multiple_of((owner ^ mask) * share, share), share), :])
    return jnp.concatenate(pieces, axis=0)


def fetch(pairs, sems):
    copies = [pltpu.make_async_copy(src, dst, sems.at[i]) for i, (src, dst) in enumerate(pairs)]
    for copy in copies:
        copy.start()
    return copies


def centered(value_ref, head, value_dim):
    values = value_ref[:, features(head, value_dim)].astype(F32)
    return values - jnp.mean(values, axis=1, keepdims=True)


def first_pack_kernel(place_ref, owner_ref, decay_hbm, key_hbm, value_hbm, *refs):
    decay_ref, key_ref, value_ref, sems = refs[-4:]
    first = refs[:-4]
    count = len(first)
    rows, width = (first[0].shape[0] - TAIL) // 2, first[0].shape[1]
    place = place_ref[0] & (count - 1)
    pairs = [(decay_hbm, decay_ref), (key_hbm, key_ref), (value_hbm, value_ref)]
    copies = fetch(pairs, sems)
    down, across = iotas(rows)
    copies[0].wait()
    scales = []
    for hop in range(count):
        decay = decay_ref[pl.ds(place ^ hop, 1), :]
        after = jnp.sum(jnp.where(across > down, decay, 0.0), axis=1, keepdims=True)
        scales.append(jnp.exp(after))
        whole = jnp.exp(jnp.sum(decay, axis=1, keepdims=True))
        whole = jnp.broadcast_to(whole, (TAIL, width))
        high = whole.astype(BF16).astype(F32)
        middle = (whole - high).astype(BF16).astype(F32)
        low = whole - high - middle
        row = lax.broadcasted_iota(jnp.int32, (TAIL, width), 0)
        tail = jnp.where(row == 0, high, jnp.where(row == 1, middle, jnp.where(row == 2, low, 0.0)))
        first[hop][2 * rows :, :] = tail.astype(BF16)
    copies[1].wait()
    for hop in range(count):
        keys = key_ref[:, features(place ^ hop, width)].astype(F32)
        first[hop][0:rows, :] = (keys * scales[hop]).astype(BF16)
    copies[2].wait()
    for hop in range(count):
        values = centered(value_ref, place ^ hop, 2 * width)
        first[hop][rows : 2 * rows, :] = values[:, :width].astype(BF16)


def second_pack_kernel(place_ref, owner_ref, decay_hbm, query_hbm, value_hbm, *refs, owners):
    decay_ref, query_ref, value_ref, ordered, sems = refs[-5:]
    second = refs[:-5]
    count = len(second)
    rows, width = second[0].shape[0] // 2, second[0].shape[1]
    place = place_ref[0] & (count - 1)
    pairs = [(decay_hbm, decay_ref), (query_hbm, query_ref), (value_hbm, value_ref)]
    copies = fetch(pairs, sems)
    down, across = iotas(rows)
    for copy in copies[:2]:
        copy.wait()
    for hop in range(count):
        head = place ^ hop
        decay = decay_ref[pl.ds(head, 1), :]
        upto = jnp.sum(jnp.where(across <= down, decay, 0.0), axis=1, keepdims=True)
        queries = query_ref[:, features(head, width)].astype(F32)
        queries = by_owner(ordered, queries * jnp.exp(upto), owner_ref[0], owners)
        second[hop][rows : 2 * rows, :] = queries.astype(BF16)
    copies[2].wait()
    for hop in range(count):
        values = centered(value_ref, place ^ hop, 2 * width)
        second[hop][0:rows, :] = values[:, width:].astype(BF16)


def block_decay(message_ref):
    tail = message_ref[message_ref.shape[0] - TAIL :, :].astype(F32)
    return tail[0:1] + tail[1:2] + tail[2:3]


def outer(keys, values):
    return lax.dot_general(keys, values, (((0,), (0,)), ((), ())), preferred_element_type=F32)


def total_state(place, first, values, rows):
    decays = [block_decay(message) for message in first]
    total = None
    for hop, message in enumerate(first):
        scale = None
        for other in range(len(first)):
            if other != hop:
                factor = jnp.where((place ^ other) > (place ^ hop), decays[other], 1.0)
                scale = factor if scale is None else scale * factor
        term = outer(message[0:rows, :], values[hop])
        term = term if scale is None else term * scale
        total = term if total is None else total + term
    return total


def first_state_kernel(place_ref, *refs, rows):
    first, (state_ref, whole_ref) = refs[:-2], refs[-2:]
    values = [message[rows : 2 * rows, :] for message in first]
    state_ref[...] = total_state(place_ref[0] & (len(first) - 1), first, values, rows).astype(BF16)
    whole = block_decay(first[0])
    for message in first[1:]:
        whole = whole * block_decay(message)
    whole_ref[...] = jnp.broadcast_to(whole, whole_ref.shape)


def second_state_kernel(place_ref, token_ref, *refs, rows):
    count = (len(refs) - 1) // 2
    first, second, state_ref = refs[:count], refs[count : 2 * count], refs[-1]
    values = [message[0:rows, :] for message in second]
    state_ref[...] = total_state(place_ref[0] & (len(first) - 1), first, values, rows).astype(BF16)


def group_kernel(place_ref, *refs, rows):
    count = (len(refs) - 6) // 2
    first, second = refs[:count], refs[count : 2 * count]
    left_ref, right_ref, scaled_ref, states, earlier, decays = refs[2 * count :]
    width = first[0].shape[1]
    place = place_ref[0] & (count - 1)
    for hop in range(count):
        block = place ^ hop
        decays[block] = jnp.broadcast_to(block_decay(first[hop]), decays.shape[1:])
        keys = first[hop][0:rows, :]
        states[block, :, 0:width] = outer(keys, first[hop][rows : 2 * rows, :])
        states[block, :, width : 2 * width] = outer(keys, second[hop][0:rows, :])
    whole = jnp.ones((1, width), F32)
    for block in range(count):
        if block == 0:
            earlier[0] = jnp.zeros(earlier.shape[1:], BF16)
        elif block == 1:
            total = states[0]
            earlier[1] = total.astype(BF16)
        else:
            total = total * jnp.concatenate([decay, decay], axis=1) + states[block - 1]
            earlier[block] = total.astype(BF16)
        decay = decays[block][0:1]
        decays[block] = jnp.broadcast_to(whole, decays.shape[1:])
        whole = whole * decay
    for hop in range(count):
        block = place ^ hop
        queries = second[hop][rows : 2 * rows, :]
        here = slice(hop * rows, (hop + 1) * rows)
        part = jnp.dot(queries, earlier[block], preferred_element_type=F32)
        left_ref[here, :] = part[:, 0:width]
        right_ref[here, :] = part[:, width : 2 * width]
        scaled_ref[here, :] = (queries.astype(F32) * decays[block][0:1]).astype(BF16)


def cross_kernel(place_ref, state_ref, scaled_ref, part_ref, *out_refs):
    rows = out_refs[0].shape[0]
    carried = jnp.dot(scaled_ref[...], state_ref[...], preferred_element_type=F32)
    total = part_ref[...] + jnp.where(place_ref[0] < len(out_refs), 0.0, carried)
    for hop, out_ref in enumerate(out_refs):
        out_ref[...] = total[hop * rows : (hop + 1) * rows, :].astype(BF16)


def block_kernel(owner_ref, *refs, owners):
    _, decay_hbm, query_hbm, key_hbm, value_hbm, gate_hbm, inner_ref, swish_ref, token_ref = refs[:9]
    decay_ref, query_ref, key_ref, value_ref, gate_ref, ordered, sems = refs[9:]
    rows = query_ref.shape[0]
    heads = decay_ref.shape[0]
    key_dim, value_dim = query_ref.shape[1] // heads, value_ref.shape[1] // heads
    copies = fetch(
        [
            (decay_hbm, decay_ref),
            (query_hbm, query_ref),
            (key_hbm, key_ref),
            (value_hbm, value_ref),
            (gate_hbm, gate_ref),
        ],
        sems,
    )
    down, across = iotas(rows)
    causal = across <= down
    for copy in copies:
        copy.wait()
    for head in range(heads):
        decay = decay_ref[head : head + 1, :]
        column = jnp.sum(jnp.where(causal, decay, 0.0), axis=1, keepdims=True)
        line = jnp.sum(jnp.where(across == down, column, 0.0), axis=0, keepdims=True)
        table = jnp.where(causal, jnp.exp(jnp.where(causal, column - line, 0.0)), 0.0)
        keys = slice(head * key_dim, (head + 1) * key_dim)
        here = slice(head * value_dim, (head + 1) * value_dim)
        scores = lax.dot_general(
            query_ref[:, keys], key_ref[:, keys], (((1,), (1,)), ((), ())), preferred_element_type=F32
        )
        inner = jnp.dot((scores * table).astype(BF16), value_ref[:, here], preferred_element_type=F32)
        inner_ref[:, here] = by_owner(ordered.at[0], inner, owner_ref[0], owners)
        gate = gate_ref[:, here].astype(F32)
        swish_ref[:, here] = by_owner(ordered.at[1], gate / (1.0 + jnp.exp(-gate)), owner_ref[0], owners)
    token_ref[...] = jnp.zeros_like(token_ref)


def mix(place_ref, inner_ref, swish_ref, part_refs, hop, group):
    value_dim = sum(part_ref.shape[1] for part_ref in part_refs)
    here = features((place_ref[0] & (group - 1)) ^ hop, value_dim)
    part = jnp.concatenate([part_ref[...] for part_ref in part_refs], axis=1)
    retained = inner_ref[:, here] + part.astype(F32)
    mean = jnp.mean(retained, axis=1, keepdims=True)
    centred = retained - mean
    variance = jnp.mean(centred * centred, axis=1, keepdims=True)
    return centred * lax.rsqrt(variance + 1e-05) * swish_ref[:, here]


def head_product(place_ref, rows, weight_ref, hop, group, start, tile):
    depth = rows.shape[1]
    return jnp.dot(
        rows,
        weight_ref[features((place_ref[0] & (group - 1)) ^ hop, depth), start : start + tile],
        preferred_element_type=F32,
    )


def add_head_kernel(*refs, hop, group, summed):
    place_ref, inner_ref, swish_ref, weight_ref = refs[:4]
    before, part_refs = refs[4 : 4 + summed], refs[4 + summed : -2]
    total_ref, mixed = refs[-2:]
    mixed[...] = mix(place_ref, inner_ref, swish_ref, part_refs, hop, group)
    rows = mixed[...].astype(BF16)
    width = total_ref.shape[1]
    tile = min(512, width)
    for start in range(0, width, tile):
        here = slice(start, start + tile)
        term = head_product(place_ref, rows, weight_ref, hop, group, start, tile)
        total_ref[:, here] = before[0][:, here] + term if before else term


def finish_part(place_ref, rows, weight_ref, totals, send_ref, keep_ref, offset, late, group):
    half, width = send_ref.shape
    tile = min(512, width)
    for start in range(0, width, tile):
        here = slice(start, start + tile)
        there = offset + start
        terms = [
            head_product(place_ref, rows_ref[...], weight_ref, hop, group, there, tile)
            for hop, rows_ref in zip(late, rows)
        ]
        terms += [total_ref[:, there : there + tile] for total_ref in totals]
        out = functools.reduce(jnp.add, terms)
        send_ref[:, here] = out[:half].astype(BF16)
        keep_ref[:, here] = out[half:].astype(BF16)


def first_part_kernel(*refs, late, group, summed):
    place_ref, inner_ref, swish_ref, weight_ref = refs[:4]
    count = len(late)
    totals, part_refs = refs[4 : 4 + summed], refs[4 + summed : -2 - count]
    send_ref, keep_ref = refs[-2 - count], refs[-1 - count]
    rows = refs[-count:]
    each = len(part_refs) // count
    for at, (hop, rows_ref) in enumerate(zip(late, rows)):
        rows_ref[...] = mix(place_ref, inner_ref, swish_ref, part_refs[at * each : (at + 1) * each], hop, group).astype(BF16)
    finish_part(place_ref, rows, weight_ref, totals, send_ref, keep_ref, 0, late, group)


def other_part_kernel(place_ref, weight_ref, *refs, offset, late, group):
    count = len(late)
    send_ref, keep_ref = refs[-2:]
    finish_part(place_ref, refs[:count], weight_ref, refs[count:-2], send_ref, keep_ref, offset, late, group)


def swap(value, axis, size, mask):
    return lax.ppermute(value, axis, [(i, i ^ mask) for i in range(size)])


def swaps(values, axis, size):
    return [swap(values[hop], axis, size, hop) for hop in range(1, len(values))]


def carried_into(state, whole, axis, size, group):
    def shift(value, by):
        return lax.ppermute(value, axis, [(i, (i + by * group) % size) for i in range(size)])

    groups = size // group
    if groups == 1:
        return state
    got = shift(state, 1)
    if groups == 2:
        return got
    first = lax.axis_index(axis) < group
    total, product = jnp.where(first, 0.0, got.astype(F32)), jnp.where(first, 1.0, shift(whole, 1))
    by = 1
    while by < groups - 1:
        none = lax.axis_index(axis) < by * group
        earlier, before = shift(total.astype(BF16), by), shift(product, by)
        total = total + jnp.where(none, 0.0, product[0:1] * earlier.astype(F32))
        product = product * jnp.where(none, 1.0, before)
        by *= 2
    return total.astype(BF16)


def reduce_over(send, keep, axis, size):
    keep = keep.astype(F32)
    mask = 1
    while mask < size:
        keep = keep + swap(send.astype(BF16), axis, size, mask).astype(F32)
        mask *= 2
        if mask < size:
            half = keep.shape[0] // 2
            send, keep = keep[:half], keep[half:]
    return keep.astype(BF16)


def local(query, key, value, gate, decay, weight, *, ctx, head):
    rows = query.shape[0]
    heads = decay.shape[0]
    key_dim = query.shape[1] // heads
    value_dim = value.shape[1] // heads
    depth, width = weight.shape
    group = heads
    me = lax.axis_index("ctx")
    place = me.astype(jnp.int32).reshape(1)
    owner = lax.axis_index("head").astype(jnp.int32).reshape(1)
    shape = jax.ShapeDtypeStruct

    def after(value):
        return lax.optimization_barrier((decay, value))[0]

    first = pl.pallas_call(
        first_pack_kernel,
        out_shape=[shape((2 * rows + TAIL, key_dim), BF16)] * group,
        in_specs=[SMEM] * 2 + [HBM] * 3,
        out_specs=[VMEM] * group,
        scratch_shapes=[
            pltpu.VMEM(decay.shape, F32),
            pltpu.VMEM(key.shape, BF16),
            pltpu.VMEM(value.shape, BF16),
            pltpu.SemaphoreType.DMA((3,)),
        ],
        compiler_params=params(8),
        cost_estimate=cost(5 * 10**9, 2**24),
        name="first_pack",
    )(place, owner, *in_hbm(decay, key, value))
    second = pl.pallas_call(
        functools.partial(second_pack_kernel, owners=head),
        out_shape=[shape((2 * rows, key_dim), BF16)] * group,
        in_specs=[SMEM] * 2 + [HBM] * 3,
        out_specs=[VMEM] * group,
        scratch_shapes=[
            pltpu.VMEM(decay.shape, F32),
            pltpu.VMEM(query.shape, BF16),
            pltpu.VMEM(value.shape, BF16),
            pltpu.VMEM((rows, key_dim), F32),
            pltpu.SemaphoreType.DMA((3,)),
        ],
        compiler_params=params(8),
        name="second_pack",
    )(place, owner, *in_hbm(after(first[0]), query, value))
    first = [first[0]] + swaps(first, "ctx", ctx)
    second = [second[0]] + swaps(second, "ctx", ctx)
    left_state, whole = pl.pallas_call(
        functools.partial(first_state_kernel, rows=rows),
        out_shape=[shape((key_dim, key_dim), BF16), shape((8, key_dim), F32)],
        in_specs=[SMEM] + [VMEM] * group,
        out_specs=[VMEM] * 2,
        compiler_params=params(8),
        cost_estimate=cost(5*10**9, 2**24),
        name="first_state",
    )(place, *first)
    left_carried = carried_into(left_state, whole, "ctx", ctx, group)

    inner, swish, token = pl.pallas_call(
        functools.partial(block_kernel, owners=head),
        out_shape=[shape(value.shape, F32)] * 2 + [shape((8, 128), F32)],
        in_specs=[SMEM, VMEM] + [HBM] * 5,
        out_specs=[VMEM] * 3,
        scratch_shapes=[
            pltpu.VMEM(decay.shape, F32),
            pltpu.VMEM(query.shape, BF16),
            pltpu.VMEM(key.shape, BF16),
            pltpu.VMEM(value.shape, BF16),
            pltpu.VMEM(gate.shape, BF16),
            pltpu.VMEM((2, rows, value_dim), F32),
            pltpu.SemaphoreType.DMA((5,)),
        ],
        compiler_params=params(8),
        cost_estimate=cost(10**9, 4 * 2**20),
        name="block_part",
    )(owner, whole, *in_hbm(decay, query, key, value, gate))

    right_state = pl.pallas_call(
        functools.partial(second_state_kernel, rows=rows),
        out_shape=shape((key_dim, key_dim), BF16),
        in_specs=[SMEM] + [VMEM] * (1 + 2 * group),
        out_specs=VMEM,
        compiler_params=params(8),
        cost_estimate=cost(5*10**9, 2**24),
        name="second_state",
    )(place, token, *first, *second)
    right_carried = carried_into(right_state, whole, "ctx", ctx, group)

    left_part, right_part, scaled = pl.pallas_call(
        functools.partial(group_kernel, rows=rows),
        out_shape=[shape((group * rows, key_dim), F32)] * 2 + [shape((group * rows, key_dim), BF16)],
        in_specs=[SMEM] + [VMEM] * (2 * group),
        out_specs=[VMEM] * 3,
        scratch_shapes=[
            pltpu.VMEM((group, key_dim, value_dim), F32),
            pltpu.VMEM((group, key_dim, value_dim), BF16),
            pltpu.VMEM((group, 8, key_dim), F32),
        ],
        compiler_params=params(8),
        cost_estimate=cost(10**9, 4 * 2**20),
        name="group_part",
    )(place, *first, *second)

    def cross(carried, part, name):
        parts = pl.pallas_call(
            cross_kernel,
            out_shape=[shape((rows, key_dim), BF16)] * group,
            in_specs=[SMEM] + [VMEM] * 3,
            out_specs=[VMEM] * group,
            compiler_params=params(8),
            name=name,
        )(place, carried, scaled, part)
        return [parts[0]] + swaps(parts, "ctx", ctx)

    left_parts = cross(left_carried, left_part, "left_cross")
    right_parts = cross(right_carried, right_part, "right_cross")
    inner, left_parts = lax.optimization_barrier((inner, left_parts))
    parts = list(zip(left_parts, right_parts))
    hops = [0, *range(2, group), *range(1, min(2, group))]
    late = hops[-1:]
    total = []
    for hop in hops[:-1]:
        total = [
            pl.pallas_call(
                functools.partial(add_head_kernel, hop=hop, group=group, summed=len(total)),
                out_shape=shape((rows, width), F32),
                in_specs=[SMEM] + [VMEM] * (3 + len(total) + len(parts[hop])),
                out_specs=VMEM,

                scratch_shapes=[pltpu.VMEM((rows, value_dim), F32)],
                compiler_params=params(4),
                name="add_head",
            )(place, inner, swish, weight, *total, *parts[hop])
        ]
    late_parts = [piece for hop in late for piece in parts[hop]]
    outs = []
    offset = 0
    for part, columns in enumerate((width * 3 // 8, width * 5 // 8)):
        halves = [shape((rows // 2, columns), BF16)] * 2
        if part == 0:
            send, keep, *last_rows = pl.pallas_call(
                functools.partial(first_part_kernel, late=late, group=group, summed=len(total)),
                out_shape=halves + [shape((rows, value_dim), BF16)] * len(late),
                in_specs=[SMEM] + [VMEM] * (3 + len(total) + len(late_parts)),
                out_specs=[VMEM] * (2 + len(late)),
                compiler_params=params(4),
                name="first_part",
            )(place, inner, swish, weight, *total, *late_parts)
        else:
            send, keep = pl.pallas_call(
                functools.partial(other_part_kernel, offset=offset, late=late, group=group),
                out_shape=halves,
                in_specs=[SMEM] + [VMEM] * (1 + len(late) + len(total)),
                out_specs=[VMEM] * 2,
                compiler_params=params(4),
                name="other_part",
            )(place, weight, *last_rows, *total)
        outs.append(reduce_over(send, keep, "head", head))
        offset += columns
    return jnp.concatenate(outs, axis=1)


def solution(mesh):
    in_specs = (
        P("ctx", "head"),
        P("ctx", "head"),
        P("ctx", "head"),
        P("ctx", "head"),
        P("head", "ctx"),
        P("head", None),
    )
    out_specs = P(("ctx", "head"), None)
    body = functools.partial(local, ctx=mesh.shape["ctx"], head=mesh.shape["head"])
    return jax.shard_map(body, mesh=mesh, in_specs=in_specs, out_specs=out_specs, check_vma=False)
```
